1024 devices in a mesh: occ: 64 (over z_hi, x, y), vir: 16 (over z_lo, core).
Axes of the slice: x: 4, y: 8, z: 16 (z_hi: 2, z_lo: 8; z = z_hi * 8 + z_lo), core: 2. Of those that a mesh axis runs over, the one named last changes fastest.
Arguments:
- amplitudes: float32 [65536, 4096], P('occ', 'vir'), may hold values from -6 to 6
- integrals: float32 [4096, 4096], P('vir'), may hold values from -0.25 to 0.25
- occ_irrep: int32 [256], replicated, may hold values from 0 to 7
- vir_irrep: int32 [64], replicated, may hold values from 0 to 7, as said below
- tile_map: int32 [64, 32], P('occ', 'vir'), may hold values 0 or 1
Outputs:
- residual: float32 [65536, 4096], P('occ', 'vir')
The draws below stay inside these ranges and needn't reach their ends.
Inputs may be any that keep to these rules, and one draw needn't show every extreme that they name: `vir_irrep`: each irrep labels exactly 8 of the virtual orbitals.
All inputs are finite; a program needn't handle non-finite values. No bound on the sum of `tile_map` on one device may be relied on, other than what follows from the above.
Results may differ from the reference program's by a relative error of at most 0.000073.
Values sent between devices are 32-bit elements; how exact they have to be, the bound alone decides.
No kernel may reach another device: no remote copies, remote signals or barrier semaphores. Data moves between devices by JAX's collectives and lax.ppermute only.
A program may use at most 64 MiB of HBM per device.

```python
import jax
import jax.numpy as jnp
from jax import lax

OI_DEV = 4
NVW = 64
TILE = 128
NOCC = 256
NIJ = 65536
NAB = 4096
N_OCC = 64


def draw_vir_irrep(key, part):
    key = jax.random.fold_in(key, 11)
    labels = jnp.arange(NVW, dtype=jnp.int32) % 8
    return jax.random.permutation(key, labels).astype(jnp.int32)


def set_ends(drawn, key, smallest, high):
    spot = [jax.random.randint(jax.random.fold_in(key, axis), (), 0, length) for axis, length in enumerate(drawn.shape)]
    widest = drawn.shape.index(max(drawn.shape))
    neighbour = spot[:widest] + [(spot[widest] + 1) % drawn.shape[widest]] + spot[widest + 1:]
    return drawn.at[tuple(spot)].set(smallest).at[tuple(neighbour)].set(high)


def levels(key, shape, cuts, least, largest):
    level = 1.0
    for dim, shards_of in cuts:
        steps = jax.random.uniform(jax.random.fold_in(jax.random.fold_in(key, 6), dim), (shards_of,), jnp.float32, least / len(cuts), largest / len(cuts))
        level = level * jnp.repeat(jnp.exp(steps), shape[dim] // shards_of).reshape((-1,) + (1,) * (len(shape) - 1 - dim))
    return level


def noise(key, dims, spread, reach, pieces=(), kind=jnp.bfloat16):
    values = spread * jax.random.normal(key, dims, jnp.float32)
    if pieces:
        values = values * levels(key, dims, pieces, -0.22, 0.18)
    return jnp.clip(values, -reach, reach).astype(kind)


def setup_inputs(seed: int = 0) -> dict:
    keys = jax.random.split(jax.random.key(seed), 6)
    return {
        "amplitudes": noise(keys[0], (NIJ, NAB), 1.0, 6.0, ((0, 64), (1, 16)), jnp.float32),
        "integrals": noise(keys[1], (NAB, NAB), (NAB // 8) ** -0.5, 0.25, ((0, 16),), jnp.float32),
        "occ_irrep": set_ends(jax.random.randint(keys[2], (NOCC,), 0, 8), jax.random.fold_in(keys[2], 1), 0, 7).astype(jnp.int32),
        "vir_irrep": draw_vir_irrep(jax.random.fold_in(keys[5], 71), 0),
        "tile_map": set_ends((jax.random.randint(keys[4], (N_OCC, NAB // TILE), 0, 4) < 3).astype(jnp.int32), jax.random.fold_in(keys[4], 1), 0, 1),
    }


def reference(amplitudes, integrals, occ_irrep, vir_irrep, tile_map):
    nocc = occ_irrep.shape[0]
    sym_ij = jnp.bitwise_xor(occ_irrep[:, None], occ_irrep[None, :]).reshape(-1)
    sym_cd = jnp.bitwise_xor(vir_irrep[:, None], vir_irrep[None, :]).reshape(-1)
    tiles = jnp.repeat(jnp.repeat(tile_map, OI_DEV * nocc, axis=0), TILE, axis=1)
    keep = jnp.logical_and(sym_ij[:, None] == sym_cd[None, :], tiles == 1)
    amps = jnp.where(keep, amplitudes, jnp.float32(0.0))
    panel = jnp.where(sym_cd[:, None] == sym_cd[None, :], integrals, jnp.float32(0.0))
    ladder = jnp.dot(amps, panel, precision=lax.Precision.HIGHEST, preferred_element_type=jnp.float32)
    four = ladder.reshape(nocc, nocc, NVW, NVW)
    result = four - four.transpose(1, 0, 2, 3) - four.transpose(0, 1, 3, 2) + four.transpose(1, 0, 3, 2)
    return result.reshape(nocc * nocc, NVW * NVW)
```

```python
import functools

import jax
import jax.numpy as jnp
from jax import lax
from jax.experimental import pallas as pl
from jax.experimental.pallas import tpu as pltpu
from jax.sharding import PartitionSpec as P

F32, BF16, I32 = jnp.float32, jnp.bfloat16, jnp.int32
CLASSES = 8
RANKS = 8
GROUP = 4
CHUNK = 512
VMEM = 48 * 1024 * 1024


def iota(shape, dim):
    return lax.broadcasted_iota(I32, shape, dim)


def pieces(value, count):
    out = []
    for step in range(count):
        part = value.astype(BF16)
        out.append(part)
        if step + 1 < count:
            value = value - part.astype(F32)
    return out


def dot(a, b):
    return lax.dot_general(a, b, (((1,), (0,)), ((), ())), preferred_element_type=F32)


def dot_nt(a, b):
    return lax.dot_general(a, b, (((1,), (1,)), ((), ())), preferred_element_type=F32)


def to_column(row):
    n = row.shape[1]
    return jnp.sum(jnp.where(iota((n, n), 0) == iota((n, n), 1), row, 0.0), axis=1, keepdims=True)


def pick_lanes(column, index):
    shape = (column.shape[0], index.shape[1])
    return jnp.sum(jnp.where(iota(shape, 0) == index, column, 0.0), axis=0, keepdims=True)


def pick_rows(row, index):
    shape = (index.shape[0], row.shape[1])
    return jnp.sum(jnp.where(iota(shape, 1) == index, row, 0.0), axis=1, keepdims=True)


def orbitals(vir_ref):
    row = vir_ref[...].astype(F32)
    col = to_column(row)
    n = row.shape[1]
    below = jnp.logical_and(col == row, iota((n, n), 1) < iota((n, n), 0))
    rank = jnp.sum(jnp.where(below, 1.0, 0.0), axis=1, keepdims=True)
    return row, col, rank


def pair_lanes(col, first, nvir, width):
    lane = iota((1, width * nvir), 1)
    one = pick_lanes(col, first + lane // nvir).astype(I32)
    two = pick_lanes(col, lane % nvir).astype(I32)
    return jnp.bitwise_xor(one, two)


def amps_kernel(amp_ref, occ_ref, vir_ref, tile_ref, own_ref, send_ref):
    nocc, nvir = occ_ref.shape[1], vir_ref.shape[1]
    width = amp_ref.shape[1] // nvir
    oi = amp_ref.shape[0] // nocc
    o, v = lax.axis_index("occ"), lax.axis_index("vir")
    _, vcol, rank = orbitals(vir_ref)
    occ = occ_ref[...].astype(F32)
    irr_j = to_column(occ).astype(I32)
    sym_cd = pair_lanes(vcol, v * width, nvir, width)
    lane = iota((1, width * nvir), 1)
    tiles = tile_ref.shape[1]
    tile = jnp.zeros_like(lane)
    for t in range(tiles):
        tile = jnp.where(lane // (width * nvir // tiles) == t, tile_ref[0, t], tile)
    sym_cd = jnp.where(tile == 1, sym_cd, -1)
    cdr, n = width * nvir, oi * width * RANKS
    rank_rows = jnp.concatenate([rank] * width, axis=0).astype(I32)
    col = iota((cdr, n), 1)
    squeeze = jnp.logical_and((col // RANKS) % width == iota((cdr, n), 0) // nvir, col % RANKS == rank_rows)
    squeeze = jnp.where(squeeze, 1.0, 0.0).astype(BF16)
    lanes = iota((nocc, n), 1) // (width * RANKS)
    own = jnp.zeros((nocc, n), F32)
    for ii in range(oi):
        irr_i = pick_rows(occ, jnp.full((1, 1), o * oi + ii, I32)).astype(I32)
        keep = jnp.bitwise_xor(irr_j, irr_i) == sym_cd
        block = jnp.where(keep, amp_ref[ii * nocc:(ii + 1) * nocc, :], 0.0)
        short = sum(dot(part, squeeze) for part in pieces(block, 3))
        own = jnp.where(lanes == ii, short, own)
    own_ref[...] = own
    devices = nocc // oi
    lanes = iota((devices, n), 1) // (width * RANKS)
    swapped = [jnp.zeros((devices, n), F32) for _ in range(oi)]
    for jj in range(oi):
        rows = own_ref[pl.ds(jj, devices, stride=oi), :]
        for ii in range(oi):
            shift = (jj - ii) % oi * (width * RANKS)
            moved = pltpu.roll(rows, shift, 1) if shift else rows
            swapped[ii] = jnp.where(lanes == jj, moved, swapped[ii])
    for ii in range(oi):
        send_ref[pl.ds(ii, devices, stride=oi), :] = swapped[ii]


def panel_kernel(steps, int_ref, vir_ref, *refs):
    outs, total = refs[:-1], refs[-1]
    q = pl.program_id(0)
    nvir = vir_ref.shape[1]
    cdr, chunk = int_ref.shape
    width = cdr // nvir
    v = lax.axis_index("vir")
    vrow, vcol, rank = orbitals(vir_ref)
    row = iota((cdr, 1), 0)
    sym_rows = jnp.bitwise_xor(pick_rows(vrow, v * width + row // nvir).astype(I32), pick_rows(vrow, row % nvir).astype(I32))
    lane = iota((1, chunk), 1)
    a, b = q * (chunk // nvir) + lane // nvir, lane % nvir
    sym_ab = jnp.bitwise_xor(pick_lanes(vcol, a).astype(I32), pick_lanes(vcol, b).astype(I32))
    plus = a * RANKS + pick_lanes(rank, b).astype(I32)
    minus = b * RANKS + pick_lanes(rank, a).astype(I32)
    n = nvir * RANKS
    dest = n // (width * RANKS * GROUP)
    col = iota((n, 1), 0)
    to = (col // (n // GROUP)) ^ (v % GROUP)
    group = ((col // (width * RANKS)) % dest) ^ (v // GROUP)
    code = (group * GROUP + to) * (width * RANKS) + col % (width * RANKS)
    fold = jnp.where(code == plus, 1.0, 0.0) - jnp.where(code == minus, 1.0, 0.0)
    fold = fold.astype(BF16)
    block = jnp.where(sym_rows == sym_ab, int_ref[...], 0.0)
    part = sum(dot_nt(fold, piece) for piece in pieces(block, 2))

    @pl.when(q == 0)
    def _():
        total[...] = part

    @pl.when(q > 0)
    def _():
        total[...] += part

    @pl.when(q == steps - 1)
    def _():
        k = CLASSES * width * RANKS
        new = iota((cdr, k), 1)
        old = iota((cdr, k), 0)
        rank_rows = jnp.concatenate([rank] * width, axis=0).astype(I32)
        order = jnp.logical_and(new // (width * RANKS) == sym_rows, (new // RANKS) % width == old // nvir)
        order = jnp.logical_and(order, new % RANKS == rank_rows)
        order = jnp.where(order, 1.0, 0.0).astype(BF16)
        placed = sum(dot(piece, order) for piece in pieces(total[...], 2))
        rows = n // GROUP
        for k, out in enumerate(outs):
            out[...] = placed[k * rows:(k + 1) * rows, :]


def antisym_kernel(own_ref, got_ref, out_ref):
    out_ref[...] = (own_ref[...] - got_ref[...]).T


def ladder_kernel(oi, *refs):
    amps, panels, occ_ref, outs = refs[:GROUP], refs[GROUP:2 * GROUP], refs[2 * GROUP], refs[2 * GROUP + 1:]
    nocc = occ_ref.shape[1]
    o = lax.axis_index("occ")
    occ = occ_ref[...].astype(F32)
    cm = amps[0].shape[0] // oi
    stacked = []
    for ref in panels:
        high, low = pieces(ref[...], 2)
        stacked.append((jnp.concatenate([high, low], axis=0), high))
    n = panels[0].shape[0]
    for ii in range(oi):
        irr_i = pick_rows(occ, jnp.full((1, 1), o * oi + ii, I32)).astype(I32)
        sym = jnp.bitwise_xor(occ_ref[...], irr_i)
        total = jnp.zeros((n, nocc), F32)
        for ref, (both, high) in zip(amps, stacked, strict=True):
            block = ref[ii * cm:(ii + 1) * cm, :]
            spread = jnp.concatenate([jnp.where(sym == s, block, 0.0) for s in range(CLASSES)], axis=0)
            upper, lower = pieces(spread, 2)
            first = dot(both, upper)
            total = total + (first[:n, :] + (first[n:, :] + dot(high, lower)))
        for d, out in enumerate(outs):
            out[ii * cm:(ii + 1) * cm, :] = total[d * cm:(d + 1) * cm, :]


def spread_kernel(oi, *refs):
    parts, occ_ref, vir_ref, out_ref = refs[:-3], refs[-3], refs[-2], refs[-1]
    nocc, nvir = occ_ref.shape[1], vir_ref.shape[1]
    width = out_ref.shape[1] // nvir
    o, v = lax.axis_index("occ"), lax.axis_index("vir")
    _, vcol, rank = orbitals(vir_ref)
    occ = occ_ref[...].astype(F32)
    irr_j = to_column(occ).astype(I32)
    sym_ab = pair_lanes(vcol, v * width, nvir, width)
    total = parts[0][...]
    for ref in parts[1:]:
        total = total + ref[...]
    total = total.T
    split = pieces(total, 3)
    n = total.shape[1]
    lane = iota((1, width * nvir), 1)
    rank_lanes = pick_lanes(rank, lane % nvir).astype(I32)
    row = iota((n, width * nvir), 0)
    open_ = jnp.logical_and((row // RANKS) % width == lane // nvir, row % RANKS == rank_lanes)
    for ii in range(oi):
        wide = jnp.where(jnp.logical_and(open_, row // (width * RANKS) == ii), 1.0, 0.0).astype(BF16)
        full = sum(dot(part, wide) for part in split)
        irr_i = pick_rows(occ, jnp.full((1, 1), o * oi + ii, I32)).astype(I32)
        keep = jnp.bitwise_xor(irr_j, irr_i) == sym_ab
        out_ref[ii * nocc:(ii + 1) * nocc, :] = jnp.where(keep, full, 0.0)


def whole(count):
    return [pl.BlockSpec(memory_space=pltpu.VMEM)] * count


def call(kernel, outs, ins, flops, interpret, smem=()):
    specs = whole(len(ins))
    for k in smem:
        specs[k] = pl.BlockSpec(memory_space=pltpu.SMEM)
    moved = sum(x.size * 4 for x in ins) + sum(x.size * 4 for x in outs)
    return pl.pallas_call(
        kernel,
        out_shape=outs,
        in_specs=specs,
        out_specs=whole(len(outs)),
        compiler_params=pltpu.CompilerParams(vmem_limit_bytes=VMEM),
        cost_estimate=pl.CostEstimate(flops=flops, bytes_accessed=moved, transcendentals=0),
        interpret=interpret,
    )(*ins)


def array(*shape):
    return jax.ShapeDtypeStruct(shape, F32)


def body(nvirdev, interpret, amplitudes, integrals, occ_irrep, vir_irrep, tile_map):
    nocc, nvir = occ_irrep.shape[0], vir_irrep.shape[0]
    oi = amplitudes.shape[0] // nocc
    cdr = amplitudes.shape[1]
    width = cdr // nvir
    cm = width * RANKS
    n = nvir * RANKS
    occ = occ_irrep.reshape(1, nocc)
    vir = vir_irrep.reshape(1, nvir)

    def swap(x, k):
        return lax.ppermute(x, "vir", [(i, i ^ k) for i in range(nvirdev)])

    own, send = call(amps_kernel, [array(nocc, oi * cm)] * 2, [amplitudes, occ, vir, tile_map], 10**9, interpret, (3,))
    got = lax.all_to_all(send.reshape(nocc // oi, oi, oi * cm), "occ", 0, 0).reshape(nocc, oi * cm)

    steps = integrals.shape[1] // CHUNK
    k = CLASSES * cm
    panels = pl.pallas_call(
        functools.partial(panel_kernel, steps),
        grid=(steps,),
        out_shape=[array(n // GROUP, k)] * GROUP,
        in_specs=[pl.BlockSpec((cdr, CHUNK), lambda q: (0, q)), pl.BlockSpec((1, nvir), lambda q: (0, 0))],
        out_specs=[pl.BlockSpec((n // GROUP, k), lambda q: (0, 0))] * GROUP,
        scratch_shapes=[pltpu.VMEM((n, cdr), F32)],
        compiler_params=pltpu.CompilerParams(vmem_limit_bytes=VMEM, dimension_semantics=("arbitrary",)),
        cost_estimate=pl.CostEstimate(flops=4 * n * cdr * nvir * nvir, bytes_accessed=8 * integrals.size, transcendentals=0),
        interpret=interpret,
    )(integrals, vir)
    panels = [x if k == 0 else swap(x, k) for k, x in enumerate(panels)]

    (anti,) = call(antisym_kernel, [array(oi * cm, nocc)], [own, got], 10**6, interpret)
    blocks = [anti if k == 0 else swap(anti, k) for k in range(GROUP)]
    far = nvirdev // GROUP
    partial_sums = call(
        functools.partial(ladder_kernel, oi), [array(oi * cm, nocc)] * far, [*blocks, *panels, occ], 2 * 10**9, interpret
    )
    sums = [x if d == 0 else swap(x, d * GROUP) for d, x in enumerate(partial_sums)]
    (out,) = call(
        functools.partial(spread_kernel, oi), [array(*amplitudes.shape)], [*sums, occ, vir], 10**9, interpret
    )
    return out


def solution(mesh, interpret=False):
    placed = (P("occ", "vir"), P("vir", None), P(), P(), P("occ", "vir"))
    return jax.shard_map(
        functools.partial(body, mesh.shape["vir"], interpret),
        mesh=mesh,
        in_specs=placed,
        out_specs=P("occ", "vir"),
        check_vma=False,
    )
```

```python
import functools

import jax
import jax.numpy as jnp
from jax import lax
from jax.experimental import pallas as pl
from jax.experimental.pallas import tpu as pltpu
from jax.sharding import PartitionSpec as P

F32, BF16, I32 = jnp.float32, jnp.bfloat16, jnp.int32
CLASSES = 8
RANKS = 8
PAIR = 2
CHUNK = 512
VMEM = 48 * 1024 * 1024


def iota(shape, dim):
    return lax.broadcasted_iota(I32, shape, dim)


def pieces(value, count):
    out = []
    for step in range(count):
        part = value.astype(BF16)
        out.append(part)
        if step + 1 < count:
            value = value - part.astype(F32)
    return out


def dot(a, b):
    return lax.dot_general(a, b, (((1,), (0,)), ((), ())), preferred_element_type=F32)


def dot_nt(a, b):
    return lax.dot_general(a, b, (((1,), (1,)), ((), ())), preferred_element_type=F32)


def to_column(row):
    n = row.shape[1]
    return jnp.sum(jnp.where(iota((n, n), 0) == iota((n, n), 1), row, 0.0), axis=1, keepdims=True)


def pick_lanes(column, index):
    shape = (column.shape[0], index.shape[1])
    return jnp.sum(jnp.where(iota(shape, 0) == index, column, 0.0), axis=0, keepdims=True)


def pick_rows(row, index):
    shape = (index.shape[0], row.shape[1])
    return jnp.sum(jnp.where(iota(shape, 1) == index, row, 0.0), axis=1, keepdims=True)


def orbitals(vir_ref):
    row = vir_ref[...].astype(F32)
    col = to_column(row)
    n = row.shape[1]
    below = jnp.logical_and(col == row, iota((n, n), 1) < iota((n, n), 0))
    rank = jnp.sum(jnp.where(below, 1.0, 0.0), axis=1, keepdims=True)
    return row, col, rank


def pair_lanes(col, first, nvir, width):
    lane = iota((1, width * nvir), 1)
    one = pick_lanes(col, first + lane // nvir).astype(I32)
    two = pick_lanes(col, lane % nvir).astype(I32)
    return jnp.bitwise_xor(one, two)


def amps_kernel(amp_hbm, occ_hbm, vir_hbm, tile_hbm, own_ref, send_ref, amp_ref, occ_ref, vir_ref, tile_ref, sems):
    nocc, nvir = occ_ref.shape[1], vir_ref.shape[1]
    width = amp_ref.shape[1] // nvir
    oi = amp_ref.shape[0] // nocc
    small = [
        pltpu.make_async_copy(a, b, sems.at[oi + k])
        for k, (a, b) in enumerate(((vir_hbm, vir_ref), (occ_hbm, occ_ref), (tile_hbm, tile_ref)))
    ]
    blocks = [
        pltpu.make_async_copy(amp_hbm.at[pl.ds(k * nocc, nocc)], amp_ref.at[pl.ds(k * nocc, nocc)], sems.at[k])
        for k in range(oi)
    ]
    for copy in small + blocks:
        copy.start()
    for copy in small:
        copy.wait()
    o, v = lax.axis_index("occ"), lax.axis_index("vir")
    _, vcol, rank = orbitals(vir_ref)
    occ = occ_ref[...].astype(F32)
    irr_j = to_column(occ).astype(I32)
    sym_cd = pair_lanes(vcol, v * width, nvir, width)
    lane = iota((1, width * nvir), 1)
    tiles = tile_ref.shape[1]
    tile = jnp.zeros_like(lane)
    for t in range(tiles):
        tile = jnp.where(lane // (width * nvir // tiles) == t, tile_ref[0, t], tile)
    sym_cd = jnp.where(tile == 1, sym_cd, -1)
    cdr, n = width * nvir, oi * width * RANKS
    rank_rows = jnp.concatenate([rank] * width, axis=0).astype(I32)
    col = iota((cdr, n), 1)
    squeeze = jnp.logical_and((col // RANKS) % width == iota((cdr, n), 0) // nvir, col % RANKS == rank_rows)
    squeeze = jnp.where(squeeze, 1.0, 0.0).astype(BF16)
    lanes = iota((nocc, n), 1) // (width * RANKS)
    own = jnp.zeros((nocc, n), F32)
    for ii in range(oi):
        irr_i = pick_rows(occ, jnp.full((1, 1), o * oi + ii, I32)).astype(I32)
        keep = jnp.bitwise_xor(irr_j, irr_i) == sym_cd
        blocks[ii].wait()
        block = jnp.where(keep, amp_ref[ii * nocc:(ii + 1) * nocc, :], 0.0)
        short = sum(dot(part, squeeze) for part in pieces(block, 3))
        own = jnp.where(lanes == ii, short, own)
    own_ref[...] = own
    devices = nocc // oi
    lanes = iota((devices, n), 1) // (width * RANKS)
    swapped = [jnp.zeros((devices, n), F32) for _ in range(oi)]
    for jj in range(oi):
        rows = own_ref[pl.ds(jj, devices, stride=oi), :]
        for ii in range(oi):
            shift = (jj - ii) % oi * (width * RANKS)
            moved = pltpu.roll(rows, shift, 1) if shift else rows
            swapped[ii] = jnp.where(lanes == jj, moved, swapped[ii])
    for ii in range(oi):
        send_ref[pl.ds(ii, devices, stride=oi), :] = swapped[ii]


def panel_kernel(int_hbm, vir_hbm, keep_ref, send_ref, int_ref, vir_ref, fold_ref, high_ref, low_ref, sems):
    nvir = vir_ref.shape[1]
    cdr = int_ref.shape[0]
    steps = int_ref.shape[1] // CHUNK
    width = cdr // nvir
    first = pltpu.make_async_copy(vir_hbm, vir_ref, sems.at[steps])
    first.start()
    copies = [
        pltpu.make_async_copy(int_hbm.at[:, pl.ds(q * CHUNK, CHUNK)], int_ref.at[:, pl.ds(q * CHUNK, CHUNK)], sems.at[q])
        for q in range(steps)
    ]
    for copy in copies:
        copy.start()
    v = lax.axis_index("vir")
    first.wait()
    vrow, vcol, rank = orbitals(vir_ref)
    row = iota((cdr, 1), 0)
    sym_rows = jnp.bitwise_xor(pick_rows(vrow, v * width + row // nvir).astype(I32), pick_rows(vrow, row % nvir).astype(I32))
    lane = iota((1, CHUNK), 1)
    b = lane % nvir
    sym_b, rank_b = pick_lanes(vcol, b).astype(I32), pick_lanes(rank, b).astype(I32)
    n = nvir * RANKS
    cm = width * RANKS
    col = iota((n, 1), 0)
    code = ((col // cm) % 4 // 2 * 4 + (col // cm) // 4 % 2 * 8 + (col // cm) % 2 + col // (n // PAIR) * 2) ^ v
    code = code * cm + col % cm
    for q in range(steps):
        a = q * (CHUNK // nvir) + lane // nvir
        sym_ab = jnp.bitwise_xor(pick_lanes(vcol, a).astype(I32), sym_b)
        sym_ab = jnp.where(a == b, -1, sym_ab)
        plus = a * RANKS + rank_b
        minus = b * RANKS + pick_lanes(rank, a).astype(I32)
        at = slice(q * CHUNK, (q + 1) * CHUNK)
        fold_ref[:, at] = jnp.where(code == plus, 1.0, jnp.where(code == minus, -1.0, 0.0)).astype(BF16)
        copies[q].wait()
        high, low = pieces(jnp.where(sym_rows == sym_ab, int_ref[:, at], 0.0), 2)
        high_ref[:, at] = high
        low_ref[:, at] = low
    total = dot_nt(fold_ref[...], high_ref[...]) + dot_nt(fold_ref[...], low_ref[...])
    k = CLASSES * cm
    new = iota((cdr, k), 1)
    rank_rows = jnp.concatenate([rank] * width, axis=0).astype(I32)
    order = jnp.logical_and(new // cm == sym_rows, (new // RANKS) % width == row // nvir)
    order = jnp.logical_and(order, new % RANKS == rank_rows)
    order = jnp.where(order, 1.0, 0.0).astype(BF16)
    placed = sum(dot(piece, order) for piece in pieces(total, 2))
    keep_ref[...] = placed[:n // PAIR, :]
    send_ref[...] = placed[n // PAIR:, :]


def antisym_kernel(own_ref, got_ref, out_ref):
    out_ref[...] = (own_ref[...] - got_ref[...]).T


def ladder_kernel(oi, one_ref, two_ref, keep_ref, got_ref, occ_ref, mine_ref, mate_ref):
    nocc = occ_ref.shape[1]
    o = lax.axis_index("occ")
    occ = occ_ref[...].astype(F32)
    cm = one_ref.shape[0] // oi
    stacked = []
    for ref in (keep_ref, got_ref):
        high, low = pieces(ref[...], 2)
        stacked.append((jnp.concatenate([high, low], axis=0), high))
    n = keep_ref.shape[0]
    for ii in range(oi):
        irr_i = pick_rows(occ, jnp.full((1, 1), o * oi + ii, I32)).astype(I32)
        sym = jnp.bitwise_xor(occ_ref[...], irr_i)
        total = jnp.zeros((n, nocc), F32)
        at = slice(ii * cm, (ii + 1) * cm)
        for ref, (both, high) in zip((one_ref, two_ref), stacked, strict=True):
            block = ref[at, :]
            spread = jnp.concatenate([jnp.where(sym == s, block, 0.0) for s in range(CLASSES)], axis=0)
            upper, lower = pieces(spread, 2)
            first = dot(both, upper)
            total = total + (first[:n, :] + (first[n:, :] + dot(high, lower)))
        for k in range(n // (2 * cm)):
            mine_ref[k, at, :] = total[2 * k * cm:(2 * k + 1) * cm, :]
            mate_ref[k, at, :] = total[(2 * k + 1) * cm:(2 * k + 2) * cm, :]


def join_kernel(mine_ref, mate_ref, *outs):
    for k, out in enumerate(outs):
        out[...] = mine_ref[k] + mate_ref[k]


def far_kernel(far_ref, got_ref, out_ref):
    out_ref[...] = far_ref[...] + got_ref[...]


def spread_kernel(oi, own_ref, near_ref, far_ref, occ_ref, vir_ref, out_ref):
    nocc, nvir = occ_ref.shape[1], vir_ref.shape[1]
    width = out_ref.shape[1] // nvir
    o, v = lax.axis_index("occ"), lax.axis_index("vir")
    _, vcol, rank = orbitals(vir_ref)
    occ = occ_ref[...].astype(F32)
    irr_j = to_column(occ).astype(I32)
    sym_ab = pair_lanes(vcol, v * width, nvir, width)
    total = (own_ref[...] + near_ref[...] + far_ref[...]).T
    split = pieces(total, 3)
    n = total.shape[1]
    lane = iota((1, width * nvir), 1)
    rank_lanes = pick_lanes(rank, lane % nvir).astype(I32)
    row = iota((n, width * nvir), 0)
    open_ = jnp.logical_and((row // RANKS) % width == lane // nvir, row % RANKS == rank_lanes)
    for ii in range(oi):
        wide = jnp.where(jnp.logical_and(open_, row // (width * RANKS) == ii), 1.0, 0.0).astype(BF16)
        full = sum(dot(part, wide) for part in split)
        irr_i = pick_rows(occ, jnp.full((1, 1), o * oi + ii, I32)).astype(I32)
        keep = jnp.bitwise_xor(irr_j, irr_i) == sym_ab
        out_ref[ii * nocc:(ii + 1) * nocc, :] = jnp.where(keep, full, 0.0)


def spec(space):
    return pl.BlockSpec(memory_space=space)


def call(kernel, outs, ins, flops, interpret, space=pltpu.VMEM, scratch=()):
    moved = sum(x.size * 4 for x in ins) + sum(x.size * 4 for x in outs)
    return pl.pallas_call(
        kernel,
        out_shape=outs,
        in_specs=[spec(space)] * len(ins),
        out_specs=[spec(pltpu.VMEM)] * len(outs),
        scratch_shapes=scratch,
        compiler_params=pltpu.CompilerParams(vmem_limit_bytes=VMEM),
        cost_estimate=pl.CostEstimate(flops=flops, bytes_accessed=moved, transcendentals=0),
        interpret=interpret,
    )(*ins)


def pinned(x):
    return pltpu.with_memory_space_constraint(x, pltpu.HBM)


def array(*shape):
    return jax.ShapeDtypeStruct(shape, F32)


def body(nvirdev, interpret, amplitudes, integrals, occ_irrep, vir_irrep, tile_map):
    nocc, nvir = occ_irrep.shape[0], vir_irrep.shape[0]
    oi = amplitudes.shape[0] // nocc
    cdr = amplitudes.shape[1]
    width = cdr // nvir
    cm = width * RANKS
    n = nvir * RANKS
    occ = occ_irrep.reshape(1, nocc)
    vir = vir_irrep.reshape(1, nvir)

    def swap(x, k):
        return lax.ppermute(x, "vir", [(i, i ^ k) for i in range(nvirdev)])

    scratch = [
        pltpu.VMEM(amplitudes.shape, F32),
        pltpu.VMEM((1, nocc), I32),
        pltpu.VMEM((1, nvir), I32),
        pltpu.SMEM(tile_map.shape, I32),
        pltpu.SemaphoreType.DMA((oi + 3,)),
    ]
    ins = [pinned(x) for x in (amplitudes, occ, vir, tile_map)]
    own, send = call(amps_kernel, [array(nocc, oi * cm)] * 2, ins, 10**9, interpret, pltpu.HBM, scratch)
    got = lax.all_to_all(send.reshape(nocc // oi, oi, oi * cm), "occ", 0, 0).reshape(nocc, oi * cm)

    scratch = [
        pltpu.VMEM(integrals.shape, F32),
        pltpu.VMEM((1, nvir), I32),
        pltpu.VMEM((n, integrals.shape[1]), BF16),
        pltpu.VMEM(integrals.shape, BF16),
        pltpu.VMEM(integrals.shape, BF16),
        pltpu.SemaphoreType.DMA((integrals.shape[1] // CHUNK + 1,)),
    ]
    outs = [array(n // PAIR, CLASSES * cm)] * 2
    keep, give = call(panel_kernel, outs, [pinned(integrals), pinned(vir)], 4 * 10**9, interpret, pltpu.HBM, scratch)
    given = swap(give, 2)

    one = array(oi * cm, nocc)
    (anti,) = call(antisym_kernel, [one], [own, got], 10**6, interpret)
    far = nvirdev // 4
    mine, mate = call(
        functools.partial(ladder_kernel, oi),
        [array(far, oi * cm, nocc)] * 2,
        [anti, swap(anti, 2), keep, given, occ],
        2 * 10**9,
        interpret,
    )
    sums = call(join_kernel, [one] * far, [mine, swap(mate, 1)], 10**6, interpret)
    (far,) = call(far_kernel, [one], [sums[2], swap(sums[3], 4)], 10**6, interpret)
    far, near = swap(far, 8), swap(sums[1], 4)
    (out,) = call(
        functools.partial(spread_kernel, oi), [array(*amplitudes.shape)], [sums[0], near, far, occ, vir], 10**9, interpret
    )
    return out


def solution(mesh, interpret=False):
    placed = (P("occ", "vir"), P("vir", None), P(), P(), P("occ", "vir"))
    return jax.shard_map(
        functools.partial(body, mesh.shape["vir"], interpret),
        mesh=mesh,
        in_specs=placed,
        out_specs=P("occ", "vir"),
        check_vma=False,
    )
```

```python
import functools

import jax
import jax.numpy as jnp
from jax import lax
from jax.experimental import pallas as pl
from jax.experimental.pallas import tpu as pltpu
from jax.sharding import PartitionSpec as P

F32, BF16, I32 = jnp.float32, jnp.bfloat16, jnp.int32
CLASSES = 8
RANKS = 8
PAIR = 2
CHUNK = 512
VMEM = 48 * 1024 * 1024


def iota(shape, dim):
    return lax.broadcasted_iota(I32, shape, dim)


def pieces(value, count):
    out = []
    for step in range(count):
        part = value.astype(BF16)
        out.append(part)
        if step + 1 < count:
            value = value - part.astype(F32)
    return out


def dot(a, b):
    return lax.dot_general(a, b, (((1,), (0,)), ((), ())), preferred_element_type=F32)


def dot_nt(a, b):
    return lax.dot_general(a, b, (((1,), (1,)), ((), ())), preferred_element_type=F32)


def to_column(row):
    n = row.shape[1]
    return jnp.sum(jnp.where(iota((n, n), 0) == iota((n, n), 1), row, 0.0), axis=1, keepdims=True)


def pick_lanes(column, index):
    shape = (column.shape[0], index.shape[1])
    return jnp.sum(jnp.where(iota(shape, 0) == index, column, 0.0), axis=0, keepdims=True)


def pick_rows(row, index):
    shape = (index.shape[0], row.shape[1])
    return jnp.sum(jnp.where(iota(shape, 1) == index, row, 0.0), axis=1, keepdims=True)


def orbitals(vir_ref):
    row = vir_ref[...].astype(F32)
    col = to_column(row)
    n = row.shape[1]
    below = jnp.logical_and(col == row, iota((n, n), 1) < iota((n, n), 0))
    rank = jnp.sum(jnp.where(below, 1.0, 0.0), axis=1, keepdims=True)
    return row, col, rank


def pair_lanes(col, first, nvir, width):
    lane = iota((1, width * nvir), 1)
    one = pick_lanes(col, first + lane // nvir).astype(I32)
    two = pick_lanes(col, lane % nvir).astype(I32)
    return jnp.bitwise_xor(one, two)


def amps_kernel(amp_hbm, occ_hbm, vir_hbm, tile_hbm, own_ref, stay_ref, hop_ref, amp_ref, occ_ref, vir_ref, tile_ref, send_ref, sems):
    nocc, nvir = occ_ref.shape[1], vir_ref.shape[1]
    width = amp_ref.shape[1] // nvir
    oi = amp_ref.shape[0] // nocc
    small = [
        pltpu.make_async_copy(a, b, sems.at[oi + k])
        for k, (a, b) in enumerate(((vir_hbm, vir_ref), (occ_hbm, occ_ref), (tile_hbm, tile_ref)))
    ]
    blocks = [
        pltpu.make_async_copy(amp_hbm.at[pl.ds(k * nocc, nocc)], amp_ref.at[pl.ds(k * nocc, nocc)], sems.at[k])
        for k in range(oi)
    ]
    for copy in small + blocks:
        copy.start()
    for copy in small:
        copy.wait()
    o, v = lax.axis_index("occ"), lax.axis_index("vir")
    _, vcol, rank = orbitals(vir_ref)
    occ = occ_ref[...].astype(F32)
    irr_j = to_column(occ).astype(I32)
    sym_cd = pair_lanes(vcol, v * width, nvir, width)
    lane = iota((1, width * nvir), 1)
    tiles = tile_ref.shape[1]
    tile = jnp.zeros_like(lane)
    for t in range(tiles):
        tile = jnp.where(lane // (width * nvir // tiles) == t, tile_ref[0, t], tile)
    sym_cd = jnp.where(tile == 1, sym_cd, -1)
    cdr, n = width * nvir, oi * width * RANKS
    rank_rows = jnp.concatenate([rank] * width, axis=0).astype(I32)
    col = iota((cdr, n), 1)
    squeeze = jnp.logical_and((col // RANKS) % width == iota((cdr, n), 0) // nvir, col % RANKS == rank_rows)
    squeeze = jnp.where(squeeze, 1.0, 0.0).astype(BF16)
    lanes = iota((nocc, n), 1) // (width * RANKS)
    own = jnp.zeros((nocc, n), F32)
    for ii in range(oi):
        irr_i = pick_rows(occ, jnp.full((1, 1), o * oi + ii, I32)).astype(I32)
        keep = jnp.bitwise_xor(irr_j, irr_i) == sym_cd
        blocks[ii].wait()
        block = jnp.where(keep, amp_ref[ii * nocc:(ii + 1) * nocc, :], 0.0)
        short = sum(dot(part, squeeze) for part in pieces(block, 3))
        own = jnp.where(lanes == ii, short, own)
    own_ref[...] = own
    devices = nocc // oi
    lanes = iota((devices, n), 1) // (width * RANKS)
    swapped = [jnp.zeros((devices, n), F32) for _ in range(oi)]
    for jj in range(oi):
        rows = own_ref[pl.ds(jj, devices, stride=oi), :]
        for ii in range(oi):
            shift = (jj - ii) % oi * (width * RANKS)
            moved = pltpu.roll(rows, shift, 1) if shift else rows
            swapped[ii] = jnp.where(lanes == jj, moved, swapped[ii])
    for ii in range(oi):
        send_ref[pl.ds(ii, devices, stride=oi), :] = swapped[ii]
    rows = nocc // 2
    high = o // (devices // 2)
    stay_ref[...] = jnp.where(high == 0, send_ref[:rows, :], send_ref[rows:, :])
    hop_ref[...] = jnp.where(high == 0, send_ref[rows:, :], send_ref[:rows, :])


def panel_kernel(int_hbm, vir_hbm, keep_ref, send_ref, int_ref, vir_ref, fold_ref, high_ref, low_ref, sems):
    nvir = vir_ref.shape[1]
    cdr = int_ref.shape[0]
    steps = int_ref.shape[1] // CHUNK
    width = cdr // nvir
    first = pltpu.make_async_copy(vir_hbm, vir_ref, sems.at[steps])
    first.start()
    copies = [
        pltpu.make_async_copy(int_hbm.at[:, pl.ds(q * CHUNK, CHUNK)], int_ref.at[:, pl.ds(q * CHUNK, CHUNK)], sems.at[q])
        for q in range(steps)
    ]
    for copy in copies:
        copy.start()
    v = lax.axis_index("vir")
    first.wait()
    vrow, vcol, rank = orbitals(vir_ref)
    row = iota((cdr, 1), 0)
    sym_rows = jnp.bitwise_xor(pick_rows(vrow, v * width + row // nvir).astype(I32), pick_rows(vrow, row % nvir).astype(I32))
    lane = iota((1, CHUNK), 1)
    b = lane % nvir
    sym_b, rank_b = pick_lanes(vcol, b).astype(I32), pick_lanes(rank, b).astype(I32)
    n = nvir * RANKS
    cm = width * RANKS
    col = iota((n, 1), 0)
    code = ((col // cm) % 4 // 2 * 4 + (col // cm) // 4 % 2 * 8 + (col // cm) % 2 + col // (n // PAIR) * 2) ^ v
    code = code * cm + col % cm
    for q in range(steps):
        a = q * (CHUNK // nvir) + lane // nvir
        sym_ab = jnp.bitwise_xor(pick_lanes(vcol, a).astype(I32), sym_b)
        sym_ab = jnp.where(a == b, -1, sym_ab)
        plus = a * RANKS + rank_b
        minus = b * RANKS + pick_lanes(rank, a).astype(I32)
        at = slice(q * CHUNK, (q + 1) * CHUNK)
        fold_ref[:, at] = jnp.where(code == plus, 1.0, jnp.where(code == minus, -1.0, 0.0)).astype(BF16)
        copies[q].wait()
        high, low = pieces(jnp.where(sym_rows == sym_ab, int_ref[:, at], 0.0), 2)
        high_ref[:, at] = high
        low_ref[:, at] = low
    total = dot_nt(fold_ref[...], high_ref[...]) + dot_nt(fold_ref[...], low_ref[...])
    k = CLASSES * cm
    new = iota((cdr, k), 1)
    rank_rows = jnp.concatenate([rank] * width, axis=0).astype(I32)
    order = jnp.logical_and(new // cm == sym_rows, (new // RANKS) % width == row // nvir)
    order = jnp.logical_and(order, new % RANKS == rank_rows)
    order = jnp.where(order, 1.0, 0.0).astype(BF16)
    placed = sum(dot(piece, order) for piece in pieces(total, 2))
    keep_ref[...] = placed[:n // PAIR, :]
    send_ref[...] = placed[n // PAIR:, :]


def merge_kernel(oi, stay_ref, hop_ref, out_ref):
    half = stay_ref.shape[0] // oi
    for k, ref in enumerate((stay_ref, hop_ref)):
        for b in range(oi):
            out_ref[pl.ds(k * oi + b, half, stride=2 * oi), :] = ref[pl.ds(b, half, stride=oi), :]


def antisym_kernel(oi, own_ref, got_ref, out_ref, diff_ref):
    rows = own_ref.shape[0] // 2
    half = rows // oi
    high = lax.axis_index("occ") // half
    for b in range(oi):
        same = got_ref[pl.ds(b, half, stride=2 * oi), :]
        other = got_ref[pl.ds(oi + b, half, stride=2 * oi), :]
        for h in range(2):
            at = pl.ds(h * rows + b, half, stride=oi)
            diff_ref[at, :] = own_ref[at, :] - jnp.where(high == h, same, other)
    out_ref[...] = diff_ref[...].T


def ladder_kernel(oi, one_ref, two_ref, keep_ref, got_ref, occ_ref, mine_ref, mate_ref):
    nocc = occ_ref.shape[1]
    o = lax.axis_index("occ")
    occ = occ_ref[...].astype(F32)
    cm = one_ref.shape[0] // oi
    stacked = []
    for ref in (keep_ref, got_ref):
        high, low = pieces(ref[...], 2)
        stacked.append((jnp.concatenate([high, low], axis=0), high))
    n = keep_ref.shape[0]
    for ii in range(oi):
        irr_i = pick_rows(occ, jnp.full((1, 1), o * oi + ii, I32)).astype(I32)
        sym = jnp.bitwise_xor(occ_ref[...], irr_i)
        total = jnp.zeros((n, nocc), F32)
        at = slice(ii * cm, (ii + 1) * cm)
        for ref, (both, high) in zip((one_ref, two_ref), stacked, strict=True):
            block = ref[at, :]
            spread = jnp.concatenate([jnp.where(sym == s, block, 0.0) for s in range(CLASSES)], axis=0)
            upper, lower = pieces(spread, 2)
            first = dot(both, upper)
            total = total + (first[:n, :] + (first[n:, :] + dot(high, lower)))
        for k in range(n // (2 * cm)):
            mine_ref[k, at, :] = total[2 * k * cm:(2 * k + 1) * cm, :]
            mate_ref[k, at, :] = total[(2 * k + 1) * cm:(2 * k + 2) * cm, :]


def join_kernel(mine_ref, mate_ref, *outs):
    for k, out in enumerate(outs):
        out[...] = mine_ref[k] + mate_ref[k]


def far_kernel(far_ref, got_ref, out_ref):
    out_ref[...] = far_ref[...] + got_ref[...]


def spread_kernel(oi, own_ref, near_ref, far_ref, occ_ref, vir_ref, out_ref):
    nocc, nvir = occ_ref.shape[1], vir_ref.shape[1]
    width = out_ref.shape[1] // nvir
    o, v = lax.axis_index("occ"), lax.axis_index("vir")
    _, vcol, rank = orbitals(vir_ref)
    occ = occ_ref[...].astype(F32)
    irr_j = to_column(occ).astype(I32)
    sym_ab = pair_lanes(vcol, v * width, nvir, width)
    total = (own_ref[...] + near_ref[...] + far_ref[...]).T
    split = pieces(total, 3)
    n = total.shape[1]
    lane = iota((1, width * nvir), 1)
    rank_lanes = pick_lanes(rank, lane % nvir).astype(I32)
    row = iota((n, width * nvir), 0)
    open_ = jnp.logical_and((row // RANKS) % width == lane // nvir, row % RANKS == rank_lanes)
    for ii in range(oi):
        wide = jnp.where(jnp.logical_and(open_, row // (width * RANKS) == ii), 1.0, 0.0).astype(BF16)
        full = sum(dot(part, wide) for part in split)
        irr_i = pick_rows(occ, jnp.full((1, 1), o * oi + ii, I32)).astype(I32)
        keep = jnp.bitwise_xor(irr_j, irr_i) == sym_ab
        out_ref[ii * nocc:(ii + 1) * nocc, :] = jnp.where(keep, full, 0.0)


def spec(space):
    return pl.BlockSpec(memory_space=space)


def call(kernel, outs, ins, flops, interpret, space=pltpu.VMEM, scratch=()):
    moved = sum(x.size * 4 for x in ins) + sum(x.size * 4 for x in outs)
    return pl.pallas_call(
        kernel,
        out_shape=outs,
        in_specs=[spec(space)] * len(ins),
        out_specs=[spec(pltpu.VMEM)] * len(outs),
        scratch_shapes=scratch,
        compiler_params=pltpu.CompilerParams(vmem_limit_bytes=VMEM),
        cost_estimate=pl.CostEstimate(flops=flops, bytes_accessed=moved, transcendentals=0),
        interpret=interpret,
    )(*ins)


def pinned(x):
    return pltpu.with_memory_space_constraint(x, pltpu.HBM)


def array(*shape):
    return jax.ShapeDtypeStruct(shape, F32)


def body(nvirdev, interpret, amplitudes, integrals, occ_irrep, vir_irrep, tile_map):
    nocc, nvir = occ_irrep.shape[0], vir_irrep.shape[0]
    oi = amplitudes.shape[0] // nocc
    cdr = amplitudes.shape[1]
    width = cdr // nvir
    cm = width * RANKS
    n = nvir * RANKS
    occ = occ_irrep.reshape(1, nocc)
    vir = vir_irrep.reshape(1, nvir)

    def swap(x, k):
        return lax.ppermute(x, "vir", [(i, i ^ k) for i in range(nvirdev)])

    scratch = [
        pltpu.VMEM(amplitudes.shape, F32),
        pltpu.VMEM((1, nocc), I32),
        pltpu.VMEM((1, nvir), I32),
        pltpu.SMEM(tile_map.shape, I32),
        pltpu.VMEM((nocc, oi * cm), F32),
        pltpu.SemaphoreType.DMA((oi + 3,)),
    ]
    ins = [pinned(x) for x in (amplitudes, occ, vir, tile_map)]
    half = array(nocc // 2, oi * cm)
    own, stay, hop = call(amps_kernel, [array(nocc, oi * cm), half, half], ins, 10**9, interpret, pltpu.HBM, scratch)
    devices = nocc // oi
    hop = lax.ppermute(hop, "occ", [(i, (i + devices // 2) % devices) for i in range(devices)])
    scratch = [
        pltpu.VMEM(integrals.shape, F32),
        pltpu.VMEM((1, nvir), I32),
        pltpu.VMEM((n, integrals.shape[1]), BF16),
        pltpu.VMEM(integrals.shape, BF16),
        pltpu.VMEM(integrals.shape, BF16),
        pltpu.SemaphoreType.DMA((integrals.shape[1] // CHUNK + 1,)),
    ]
    outs = [array(n // PAIR, CLASSES * cm)] * 2
    keep, give = call(panel_kernel, outs, [pinned(integrals), pinned(vir)], 4 * 10**9, interpret, pltpu.HBM, scratch)
    stay, keep = lax.optimization_barrier((stay, keep))
    given = swap(give, 2)

    (send,) = call(functools.partial(merge_kernel, oi), [array(nocc, oi * cm)], [stay, hop], 10**6, interpret)
    halves = [list(range(devices // 2)), list(range(devices // 2, devices))]
    got = lax.all_to_all(send.reshape(devices // 2, 2 * oi, oi * cm), "occ", 0, 0, axis_index_groups=halves)
    got = got.reshape(nocc, oi * cm)


    one = array(oi * cm, nocc)
    scratch = [pltpu.VMEM((nocc, oi * cm), F32)]
    (anti,) = call(functools.partial(antisym_kernel, oi), [one], [own, got], 10**6, interpret, scratch=scratch)
    far = nvirdev // 4
    mine, mate = call(
        functools.partial(ladder_kernel, oi),
        [array(far, oi * cm, nocc)] * 2,
        [anti, swap(anti, 2), keep, given, occ],
        2 * 10**9,
        interpret,
    )
    sums = call(join_kernel, [one] * far, [mine, swap(mate, 1)], 10**6, interpret)
    (far,) = call(far_kernel, [one], [sums[2], swap(sums[3], 4)], 10**6, interpret)
    far, near = swap(far, 8), swap(sums[1], 4)
    (out,) = call(
        functools.partial(spread_kernel, oi), [array(*amplitudes.shape)], [sums[0], near, far, occ, vir], 10**9, interpret
    )
    return out


def solution(mesh, interpret=False):
    placed = (P("occ", "vir"), P("vir", None), P(), P(), P("occ", "vir"))
    return jax.shard_map(
        functools.partial(body, mesh.shape["vir"], interpret),
        mesh=mesh,
        in_specs=placed,
        out_specs=P("occ", "vir"),
        check_vma=False,
    )
```

```python
import functools

import jax
import jax.numpy as jnp
from jax import lax
from jax.experimental import pallas as pl
from jax.experimental.pallas import tpu as pltpu
from jax.sharding import PartitionSpec as P

F32, BF16, I32 = jnp.float32, jnp.bfloat16, jnp.int32
CLASSES = 8
RANKS = 8
PAIR = 2
CHUNK = 512
VMEM = 48 * 1024 * 1024


def iota(shape, dim):
    return lax.broadcasted_iota(I32, shape, dim)


def pieces(value, count):
    out = []
    for step in range(count):
        part = value.astype(BF16)
        out.append(part)
        if step + 1 < count:
            value = value - part.astype(F32)
    return out


def dot(a, b):
    return lax.dot_general(a, b, (((1,), (0,)), ((), ())), preferred_element_type=F32)


def dot_nt(a, b):
    return lax.dot_general(a, b, (((1,), (1,)), ((), ())), preferred_element_type=F32)


def to_column(row):
    n = row.shape[1]
    return jnp.sum(jnp.where(iota((n, n), 0) == iota((n, n), 1), row, 0.0), axis=1, keepdims=True)


def pick_lanes(column, index):
    shape = (column.shape[0], index.shape[1])
    return jnp.sum(jnp.where(iota(shape, 0) == index, column, 0.0), axis=0, keepdims=True)


def pick_rows(row, index):
    shape = (index.shape[0], row.shape[1])
    return jnp.sum(jnp.where(iota(shape, 1) == index, row, 0.0), axis=1, keepdims=True)


def orbitals(vir_ref):
    row = vir_ref[...].astype(F32)
    col = to_column(row)
    n = row.shape[1]
    below = jnp.logical_and(col == row, iota((n, n), 1) < iota((n, n), 0))
    rank = jnp.sum(jnp.where(below, 1.0, 0.0), axis=1, keepdims=True)
    return row, col, rank


def pair_lanes(col, first, nvir, width):
    lane = iota((1, width * nvir), 1)
    one = pick_lanes(col, first + lane // nvir).astype(I32)
    two = pick_lanes(col, lane % nvir).astype(I32)
    return jnp.bitwise_xor(one, two)


def amps_kernel(amp_hbm, occ_hbm, vir_hbm, tile_hbm, own_ref, stay_ref, hop_ref, amp_ref, occ_ref, vir_ref, tile_ref, send_ref, sems):
    nocc, nvir = occ_ref.shape[1], vir_ref.shape[1]
    width = amp_ref.shape[1] // nvir
    oi = amp_ref.shape[0] // nocc
    small = [
        pltpu.make_async_copy(a, b, sems.at[oi + k])
        for k, (a, b) in enumerate(((vir_hbm, vir_ref), (occ_hbm, occ_ref), (tile_hbm, tile_ref)))
    ]
    blocks = [
        pltpu.make_async_copy(amp_hbm.at[pl.ds(k * nocc, nocc)], amp_ref.at[pl.ds(k * nocc, nocc)], sems.at[k])
        for k in range(oi)
    ]
    for copy in small + blocks:
        copy.start()
    for copy in small:
        copy.wait()
    o, v = lax.axis_index("occ"), lax.axis_index("vir")
    _, vcol, rank = orbitals(vir_ref)
    occ = occ_ref[...].astype(F32)
    irr_j = to_column(occ).astype(I32)
    sym_cd = pair_lanes(vcol, v * width, nvir, width)
    lane = iota((1, width * nvir), 1)
    tiles = tile_ref.shape[1]
    tile = jnp.zeros_like(lane)
    for t in range(tiles):
        tile = jnp.where(lane // (width * nvir // tiles) == t, tile_ref[0, t], tile)
    sym_cd = jnp.where(tile == 1, sym_cd, -1)
    cdr, n = width * nvir, oi * width * RANKS
    rank_rows = jnp.concatenate([rank] * width, axis=0).astype(I32)
    col = iota((cdr, n), 1)
    squeeze = jnp.logical_and((col // RANKS) % width == iota((cdr, n), 0) // nvir, col % RANKS == rank_rows)
    squeeze = jnp.where(squeeze, 1.0, 0.0).astype(BF16)
    lanes = iota((nocc, n), 1) // (width * RANKS)
    own = jnp.zeros((nocc, n), F32)
    for ii in range(oi):
        irr_i = pick_rows(occ, jnp.full((1, 1), o * oi + ii, I32)).astype(I32)
        keep = jnp.bitwise_xor(irr_j, irr_i) == sym_cd
        blocks[ii].wait()
        block = jnp.where(keep, amp_ref[ii * nocc:(ii + 1) * nocc, :], 0.0)
        short = sum(dot(part, squeeze) for part in pieces(block, 3))
        own = jnp.where(lanes == ii, short, own)
    own_ref[...] = own
    devices = nocc // oi
    lanes = iota((devices, n), 1) // (width * RANKS)
    swapped = [jnp.zeros((devices, n), F32) for _ in range(oi)]
    for jj in range(oi):
        rows = own_ref[pl.ds(jj, devices, stride=oi), :]
        for ii in range(oi):
            shift = (jj - ii) % oi * (width * RANKS)
            moved = pltpu.roll(rows, shift, 1) if shift else rows
            swapped[ii] = jnp.where(lanes == jj, moved, swapped[ii])
    for ii in range(oi):
        send_ref[pl.ds(ii, devices, stride=oi), :] = swapped[ii]
    rows = nocc // 2
    high = o // (devices // 2)
    stay_ref[...] = jnp.where(high == 0, send_ref[:rows, :], send_ref[rows:, :])
    hop_ref[...] = jnp.where(high == 0, send_ref[rows:, :], send_ref[:rows, :])


def panel_kernel(int_hbm, vir_hbm, keep_ref, send_ref, int_ref, vir_ref, fold_ref, high_ref, low_ref, sems):
    nvir = vir_ref.shape[1]
    cdr = int_ref.shape[0]
    steps = int_ref.shape[1] // CHUNK
    width = cdr // nvir
    first = pltpu.make_async_copy(vir_hbm, vir_ref, sems.at[steps])
    first.start()
    copies = [
        pltpu.make_async_copy(int_hbm.at[:, pl.ds(q * CHUNK, CHUNK)], int_ref.at[:, pl.ds(q * CHUNK, CHUNK)], sems.at[q])
        for q in range(steps)
    ]
    for copy in copies:
        copy.start()
    v = lax.axis_index("vir")
    first.wait()
    vrow, vcol, rank = orbitals(vir_ref)
    row = iota((cdr, 1), 0)
    sym_rows = jnp.bitwise_xor(pick_rows(vrow, v * width + row // nvir).astype(I32), pick_rows(vrow, row % nvir).astype(I32))
    lane = iota((1, CHUNK), 1)
    b = lane % nvir
    sym_b, rank_b = pick_lanes(vcol, b).astype(I32), pick_lanes(rank, b).astype(I32)
    n = nvir * RANKS
    cm = width * RANKS
    col = iota((n, 1), 0)
    code = ((col // cm) % 4 // 2 * 4 + (col // cm) // 4 % 2 * 8 + (col // cm) % 2 + col // (n // PAIR) * 2) ^ v
    code = code * cm + col % cm
    for q in range(steps):
        a = q * (CHUNK // nvir) + lane // nvir
        sym_ab = jnp.bitwise_xor(pick_lanes(vcol, a).astype(I32), sym_b)
        sym_ab = jnp.where(a == b, -1, sym_ab)
        plus = a * RANKS + rank_b
        minus = b * RANKS + pick_lanes(rank, a).astype(I32)
        at = slice(q * CHUNK, (q + 1) * CHUNK)
        fold_ref[:, at] = jnp.where(code == plus, 1.0, jnp.where(code == minus, -1.0, 0.0)).astype(BF16)
        copies[q].wait()
        high, low = pieces(jnp.where(sym_rows == sym_ab, int_ref[:, at], 0.0), 2)
        high_ref[:, at] = high
        low_ref[:, at] = low
    total = dot_nt(fold_ref[...], high_ref[...]) + dot_nt(fold_ref[...], low_ref[...])
    k = CLASSES * cm
    new = iota((cdr, k), 1)
    rank_rows = jnp.concatenate([rank] * width, axis=0).astype(I32)
    order = jnp.logical_and(new // cm == sym_rows, (new // RANKS) % width == row // nvir)
    order = jnp.logical_and(order, new % RANKS == rank_rows)
    order = jnp.where(order, 1.0, 0.0).astype(BF16)
    placed = sum(dot(piece, order) for piece in pieces(total, 2))
    keep_ref[...] = placed[:n // PAIR, :]
    send_ref[...] = placed[n // PAIR:, :]


def merge_kernel(oi, stay_ref, hop_ref, out_ref):
    half = stay_ref.shape[0] // oi
    for k, ref in enumerate((stay_ref, hop_ref)):
        for b in range(oi):
            out_ref[pl.ds(k * oi + b, half, stride=2 * oi), :] = ref[pl.ds(b, half, stride=oi), :]


def antisym_kernel(oi, own_ref, got_ref, out_ref, diff_ref):
    rows = own_ref.shape[0] // 2
    half = rows // oi
    high = lax.axis_index("occ") // half
    for b in range(oi):
        same = got_ref[pl.ds(b, half, stride=2 * oi), :]
        other = got_ref[pl.ds(oi + b, half, stride=2 * oi), :]
        for h in range(2):
            at = pl.ds(h * rows + b, half, stride=oi)
            diff_ref[at, :] = own_ref[at, :] - jnp.where(high == h, same, other)
    out_ref[...] = diff_ref[...].T


def ladder_kernel(oi, one_ref, two_ref, keep_ref, got_ref, occ_ref, mine_ref, mate_ref):
    nocc = occ_ref.shape[1]
    o = lax.axis_index("occ")
    occ = occ_ref[...].astype(F32)
    cm = one_ref.shape[0] // oi
    stacked = []
    for ref in (keep_ref, got_ref):
        high, low = pieces(ref[...], 2)
        stacked.append((jnp.concatenate([high, low], axis=0), high))
    n = keep_ref.shape[0]
    for ii in range(oi):
        irr_i = pick_rows(occ, jnp.full((1, 1), o * oi + ii, I32)).astype(I32)
        sym = jnp.bitwise_xor(occ_ref[...], irr_i)
        total = jnp.zeros((n, nocc), F32)
        at = slice(ii * cm, (ii + 1) * cm)
        for ref, (both, high) in zip((one_ref, two_ref), stacked, strict=True):
            block = ref[at, :]
            spread = jnp.concatenate([jnp.where(sym == s, block, 0.0) for s in range(CLASSES)], axis=0)
            upper, lower = pieces(spread, 2)
            first = dot(both, upper)
            total = total + (first[:n, :] + (first[n:, :] + dot(high, lower)))
        for k in range(n // (2 * cm)):
            mine_ref[k, at, :] = total[2 * k * cm:(2 * k + 1) * cm, :]
            mate_ref[k, at, :] = total[(2 * k + 1) * cm:(2 * k + 2) * cm, :]


def join_kernel(mine_ref, mate_ref, own_ref, far_ref, near_ref):
    own_ref[...] = mine_ref[0] + mate_ref[0]
    far_ref[...] = mine_ref[2] + mate_ref[2]
    near_ref[0] = mine_ref[3] + mate_ref[3]
    near_ref[1] = mine_ref[1] + mate_ref[1]


def far_kernel(far_ref, near_ref, out_ref):
    out_ref[...] = far_ref[...] + near_ref[0]


def spread_kernel(oi, own_ref, near_ref, far_ref, occ_ref, vir_ref, out_ref):
    nocc, nvir = occ_ref.shape[1], vir_ref.shape[1]
    width = out_ref.shape[1] // nvir
    o, v = lax.axis_index("occ"), lax.axis_index("vir")
    _, vcol, rank = orbitals(vir_ref)
    occ = occ_ref[...].astype(F32)
    irr_j = to_column(occ).astype(I32)
    sym_ab = pair_lanes(vcol, v * width, nvir, width)
    total = (own_ref[...] + near_ref[1] + far_ref[...]).T
    split = pieces(total, 3)
    n = total.shape[1]
    lane = iota((1, width * nvir), 1)
    rank_lanes = pick_lanes(rank, lane % nvir).astype(I32)
    row = iota((n, width * nvir), 0)
    open_ = jnp.logical_and((row // RANKS) % width == lane // nvir, row % RANKS == rank_lanes)
    for ii in range(oi):
        wide = jnp.where(jnp.logical_and(open_, row // (width * RANKS) == ii), 1.0, 0.0).astype(BF16)
        full = sum(dot(part, wide) for part in split)
        irr_i = pick_rows(occ, jnp.full((1, 1), o * oi + ii, I32)).astype(I32)
        keep = jnp.bitwise_xor(irr_j, irr_i) == sym_ab
        out_ref[ii * nocc:(ii + 1) * nocc, :] = jnp.where(keep, full, 0.0)


def spec(space):
    return pl.BlockSpec(memory_space=space)


def call(kernel, outs, ins, flops, interpret, space=pltpu.VMEM, scratch=()):
    moved = sum(x.size * 4 for x in ins) + sum(x.size * 4 for x in outs)
    return pl.pallas_call(
        kernel,
        out_shape=outs,
        in_specs=[spec(space)] * len(ins),
        out_specs=[spec(pltpu.VMEM)] * len(outs),
        scratch_shapes=scratch,
        compiler_params=pltpu.CompilerParams(vmem_limit_bytes=VMEM),
        cost_estimate=pl.CostEstimate(flops=flops, bytes_accessed=moved, transcendentals=0),
        interpret=interpret,
    )(*ins)


def pinned(x):
    return pltpu.with_memory_space_constraint(x, pltpu.HBM)


def array(*shape):
    return jax.ShapeDtypeStruct(shape, F32)


def body(nvirdev, interpret, amplitudes, integrals, occ_irrep, vir_irrep, tile_map):
    nocc, nvir = occ_irrep.shape[0], vir_irrep.shape[0]
    oi = amplitudes.shape[0] // nocc
    cdr = amplitudes.shape[1]
    width = cdr // nvir
    cm = width * RANKS
    n = nvir * RANKS
    occ = occ_irrep.reshape(1, nocc)
    vir = vir_irrep.reshape(1, nvir)

    def swap(x, k):
        return lax.ppermute(x, "vir", [(i, i ^ k) for i in range(nvirdev)])

    scratch = [
        pltpu.VMEM(amplitudes.shape, F32),
        pltpu.VMEM((1, nocc), I32),
        pltpu.VMEM((1, nvir), I32),
        pltpu.SMEM(tile_map.shape, I32),
        pltpu.VMEM((nocc, oi * cm), F32),
        pltpu.SemaphoreType.DMA((oi + 3,)),
    ]
    ins = [pinned(x) for x in (amplitudes, occ, vir, tile_map)]
    half = array(nocc // 2, oi * cm)
    own, stay, hop = call(amps_kernel, [array(nocc, oi * cm), half, half], ins, 10**9, interpret, pltpu.HBM, scratch)
    devices = nocc // oi
    hop = lax.ppermute(hop, "occ", [(i, (i + devices // 2) % devices) for i in range(devices)])
    scratch = [
        pltpu.VMEM(integrals.shape, F32),
        pltpu.VMEM((1, nvir), I32),
        pltpu.VMEM((n, integrals.shape[1]), BF16),
        pltpu.VMEM(integrals.shape, BF16),
        pltpu.VMEM(integrals.shape, BF16),
        pltpu.SemaphoreType.DMA((integrals.shape[1] // CHUNK + 1,)),
    ]
    outs = [array(n // PAIR, CLASSES * cm)] * 2
    keep, give = call(panel_kernel, outs, [pinned(integrals), pinned(vir)], 4 * 10**9, interpret, pltpu.HBM, scratch)
    stay, keep = lax.optimization_barrier((stay, keep))
    given = swap(give, 2)

    (send,) = call(functools.partial(merge_kernel, oi), [array(nocc, oi * cm)], [stay, hop], 10**6, interpret)
    halves = [list(range(devices // 2)), list(range(devices // 2, devices))]
    got = lax.all_to_all(send.reshape(devices // 2, 2 * oi, oi * cm), "occ", 0, 0, axis_index_groups=halves)
    got = got.reshape(nocc, oi * cm)


    one = array(oi * cm, nocc)
    scratch = [pltpu.VMEM((nocc, oi * cm), F32)]
    (anti,) = call(functools.partial(antisym_kernel, oi), [one], [own, got], 10**6, interpret, scratch=scratch)
    far = nvirdev // 4
    mine, mate = call(
        functools.partial(ladder_kernel, oi),
        [array(far, oi * cm, nocc)] * 2,
        [anti, swap(anti, 2), keep, given, occ],
        2 * 10**9,
        interpret,
    )
    sums, far, near = call(join_kernel, [one, one, array(2, oi * cm, nocc)], [mine, swap(mate, 1)], 10**6, interpret)
    near = swap(near, 4)
    (far,) = call(far_kernel, [one], [far, near], 10**6, interpret)
    far = swap(far, 8)
    (out,) = call(
        functools.partial(spread_kernel, oi), [array(*amplitudes.shape)], [sums, near, far, occ, vir], 10**9, interpret
    )
    return out


def solution(mesh, interpret=False):
    placed = (P("occ", "vir"), P("vir", None), P(), P(), P("occ", "vir"))
    return jax.shard_map(
        functools.partial(body, mesh.shape["vir"], interpret),
        mesh=mesh,
        in_specs=placed,
        out_specs=P("occ", "vir"),
        check_vma=False,
    )
```

```python
import functools

import jax
import jax.numpy as jnp
from jax import lax
from jax.experimental import pallas as pl
from jax.experimental.pallas import tpu as pltpu
from jax.sharding import PartitionSpec as P

F32, BF16, I32 = jnp.float32, jnp.bfloat16, jnp.int32
CLASSES = 8
RANKS = 8
PAIR = 2
CHUNK = 512
VMEM = 48 * 1024 * 1024


def iota(shape, dim):
    return lax.broadcasted_iota(I32, shape, dim)


def pieces(value, count):
    out = []
    for step in range(count):
        part = value.astype(BF16)
        out.append(part)
        if step + 1 < count:
            value = value - part.astype(F32)
    return out


def dot(a, b):
    return lax.dot_general(a, b, (((1,), (0,)), ((), ())), preferred_element_type=F32)


def dot_nt(a, b):
    return lax.dot_general(a, b, (((1,), (1,)), ((), ())), preferred_element_type=F32)


def to_column(row):
    n = row.shape[1]
    return jnp.sum(jnp.where(iota((n, n), 0) == iota((n, n), 1), row, 0.0), axis=1, keepdims=True)


def pick_lanes(column, index):
    shape = (column.shape[0], index.shape[1])
    return jnp.sum(jnp.where(iota(shape, 0) == index, column, 0.0), axis=0, keepdims=True)


def pick_rows(row, index):
    shape = (index.shape[0], row.shape[1])
    return jnp.sum(jnp.where(iota(shape, 1) == index, row, 0.0), axis=1, keepdims=True)


def orbitals(vir_ref):
    row = vir_ref[...].astype(F32)
    col = to_column(row)
    n = row.shape[1]
    below = jnp.logical_and(col == row, iota((n, n), 1) < iota((n, n), 0))
    rank = jnp.sum(jnp.where(below, 1.0, 0.0), axis=1, keepdims=True)
    return row, col, rank


def pair_lanes(col, first, nvir, width):
    lane = iota((1, width * nvir), 1)
    one = pick_lanes(col, first + lane // nvir).astype(I32)
    two = pick_lanes(col, lane % nvir).astype(I32)
    return jnp.bitwise_xor(one, two)


def amps_kernel(amp_hbm, occ_hbm, vir_hbm, tile_hbm, own_ref, stay_ref, hop_ref, amp_ref, occ_ref, vir_ref, tile_ref, send_ref, sems):
    nocc, nvir = occ_ref.shape[1], vir_ref.shape[1]
    width = amp_ref.shape[1] // nvir
    oi = amp_ref.shape[0] // nocc
    small = [
        pltpu.make_async_copy(a, b, sems.at[oi + k])
        for k, (a, b) in enumerate(((vir_hbm, vir_ref), (occ_hbm, occ_ref), (tile_hbm, tile_ref)))
    ]
    blocks = [
        pltpu.make_async_copy(amp_hbm.at[pl.ds(k * nocc, nocc)], amp_ref.at[pl.ds(k * nocc, nocc)], sems.at[k])
        for k in range(oi)
    ]
    for copy in small + blocks:
        copy.start()
    for copy in small:
        copy.wait()
    o, v = lax.axis_index("occ"), lax.axis_index("vir")
    _, vcol, rank = orbitals(vir_ref)
    occ = occ_ref[...].astype(F32)
    irr_j = to_column(occ).astype(I32)
    sym_cd = pair_lanes(vcol, v * width, nvir, width)
    lane = iota((1, width * nvir), 1)
    tiles = tile_ref.shape[1]
    tile = jnp.zeros_like(lane)
    for t in range(tiles):
        tile = jnp.where(lane // (width * nvir // tiles) == t, tile_ref[0, t], tile)
    sym_cd = jnp.where(tile == 1, sym_cd, -1)
    cdr, n = width * nvir, oi * width * RANKS
    rank_rows = jnp.concatenate([rank] * width, axis=0).astype(I32)
    col = iota((cdr, n), 1)
    squeeze = jnp.logical_and((col // RANKS) % width == iota((cdr, n), 0) // nvir, col % RANKS == rank_rows)
    squeeze = jnp.where(squeeze, 1.0, 0.0).astype(BF16)
    lanes = iota((nocc, n), 1) // (width * RANKS)
    own = jnp.zeros((nocc, n), F32)
    for ii in range(oi):
        irr_i = pick_rows(occ, jnp.full((1, 1), o * oi + ii, I32)).astype(I32)
        keep = jnp.bitwise_xor(irr_j, irr_i) == sym_cd
        blocks[ii].wait()
        block = jnp.where(keep, amp_ref[ii * nocc:(ii + 1) * nocc, :], 0.0)
        short = sum(dot(part, squeeze) for part in pieces(block, 3))
        own = jnp.where(lanes == ii, short, own)
    own_ref[...] = own
    devices = nocc // oi
    lanes = iota((devices, n), 1) // (width * RANKS)
    swapped = [jnp.zeros((devices, n), F32) for _ in range(oi)]
    for jj in range(oi):
        rows = own_ref[pl.ds(jj, devices, stride=oi), :]
        for ii in range(oi):
            shift = (jj - ii) % oi * (width * RANKS)
            moved = pltpu.roll(rows, shift, 1) if shift else rows
            swapped[ii] = jnp.where(lanes == jj, moved, swapped[ii])
    for ii in range(oi):
        send_ref[pl.ds(ii, devices, stride=oi), :] = swapped[ii]
    rows = nocc // 2
    high = o // (devices // 2)
    stay_ref[...] = jnp.where(high == 0, send_ref[:rows, :], send_ref[rows:, :])
    hop_ref[...] = jnp.where(high == 0, send_ref[rows:, :], send_ref[:rows, :])


def panel_kernel(int_hbm, vir_hbm, keep_ref, send_ref, int_ref, vir_ref, fold_ref, high_ref, low_ref, sems):
    nvir = vir_ref.shape[1]
    cdr = int_ref.shape[0]
    steps = int_ref.shape[1] // CHUNK
    width = cdr // nvir
    first = pltpu.make_async_copy(vir_hbm, vir_ref, sems.at[steps])
    first.start()
    copies = [
        pltpu.make_async_copy(int_hbm.at[:, pl.ds(q * CHUNK, CHUNK)], int_ref.at[:, pl.ds(q * CHUNK, CHUNK)], sems.at[q])
        for q in range(steps)
    ]
    for copy in copies:
        copy.start()
    v = lax.axis_index("vir")
    first.wait()
    vrow, vcol, rank = orbitals(vir_ref)
    row = iota((cdr, 1), 0)
    sym_rows = jnp.bitwise_xor(pick_rows(vrow, v * width + row // nvir).astype(I32), pick_rows(vrow, row % nvir).astype(I32))
    lane = iota((1, CHUNK), 1)
    b = lane % nvir
    sym_b, rank_b = pick_lanes(vcol, b).astype(I32), pick_lanes(rank, b).astype(I32)
    n = nvir * RANKS
    cm = width * RANKS
    col = iota((n, 1), 0)
    code = ((col // cm) % 4 // 2 * 4 + (col // cm) // 4 % 2 * 8 + (col // cm) % 2 + col // (n // PAIR) * 2) ^ v
    code = code * cm + col % cm
    for q in range(steps):
        a = q * (CHUNK // nvir) + lane // nvir
        sym_ab = jnp.bitwise_xor(pick_lanes(vcol, a).astype(I32), sym_b)
        sym_ab = jnp.where(a == b, -1, sym_ab)
        plus = a * RANKS + rank_b
        minus = b * RANKS + pick_lanes(rank, a).astype(I32)
        at = slice(q * CHUNK, (q + 1) * CHUNK)
        fold_ref[:, at] = jnp.where(code == plus, 1.0, jnp.where(code == minus, -1.0, 0.0)).astype(BF16)
        copies[q].wait()
        high, low = pieces(jnp.where(sym_rows == sym_ab, int_ref[:, at], 0.0), 2)
        high_ref[:, at] = high
        low_ref[:, at] = low
    total = dot_nt(fold_ref[...], high_ref[...]) + dot_nt(fold_ref[...], low_ref[...])
    k = CLASSES * cm
    new = iota((cdr, k), 1)
    rank_rows = jnp.concatenate([rank] * width, axis=0).astype(I32)
    order = jnp.logical_and(new // cm == sym_rows, (new // RANKS) % width == row // nvir)
    order = jnp.logical_and(order, new % RANKS == rank_rows)
    order = jnp.where(order, 1.0, 0.0).astype(BF16)
    placed = sum(dot(piece, order) for piece in pieces(total, 2))
    keep_ref[...] = placed[:n // PAIR, :]
    send_ref[...] = placed[n // PAIR:, :]


def merge_kernel(oi, stay_ref, hop_ref, out_ref):
    half = stay_ref.shape[0] // oi
    for k, ref in enumerate((stay_ref, hop_ref)):
        for b in range(oi):
            out_ref[pl.ds(k * oi + b, half, stride=2 * oi), :] = ref[pl.ds(b, half, stride=oi), :]


def antisym_kernel(oi, own_ref, got_ref, out_ref, diff_ref):
    rows = own_ref.shape[0] // 2
    half = rows // oi
    high = lax.axis_index("occ") // half
    for b in range(oi):
        same = got_ref[pl.ds(b, half, stride=2 * oi), :]
        other = got_ref[pl.ds(oi + b, half, stride=2 * oi), :]
        for h in range(2):
            at = pl.ds(h * rows + b, half, stride=oi)
            diff_ref[at, :] = own_ref[at, :] - jnp.where(high == h, same, other)
    out_ref[...] = diff_ref[...].T


def ladder_kernel(oi, part, one_ref, two_ref, keep_ref, got_ref, occ_ref, *refs):
    mine_ref, mate_ref = refs[-2:]
    nocc = occ_ref.shape[1]
    o = lax.axis_index("occ")
    occ = occ_ref[...].astype(F32)
    cm = one_ref.shape[0] // oi
    n = keep_ref.shape[0] // 2
    stacked = []
    for ref in (keep_ref, got_ref):
        high, low = pieces(ref[part * n:(part + 1) * n, :], 2)
        stacked.append((jnp.concatenate([high, low], axis=0), high))
    for ii in range(oi):
        irr_i = pick_rows(occ, jnp.full((1, 1), o * oi + ii, I32)).astype(I32)
        sym = jnp.bitwise_xor(occ_ref[...], irr_i)
        total = jnp.zeros((n, nocc), F32)
        at = slice(ii * cm, (ii + 1) * cm)
        for ref, (both, high) in zip((one_ref, two_ref), stacked, strict=True):
            block = ref[at, :]
            spread = jnp.concatenate([jnp.where(sym == s, block, 0.0) for s in range(CLASSES)], axis=0)
            upper, lower = pieces(spread, 2)
            first = dot(both, upper)
            total = total + (first[:n, :] + (first[n:, :] + dot(high, lower)))
        for k in range(n // (2 * cm)):
            mine_ref[k, at, :] = total[2 * k * cm:(2 * k + 1) * cm, :]
            mate_ref[k, at, :] = total[(2 * k + 1) * cm:(2 * k + 2) * cm, :]


def join_kernel(mine_ref, mate_ref, *outs):
    for k, out in enumerate(outs):
        out[...] = mine_ref[k] + mate_ref[k]


def far_kernel(far_ref, got_ref, out_ref):
    out_ref[...] = far_ref[...] + got_ref[...]


def spread_kernel(oi, own_ref, near_ref, far_ref, occ_ref, vir_ref, out_ref):
    nocc, nvir = occ_ref.shape[1], vir_ref.shape[1]
    width = out_ref.shape[1] // nvir
    o, v = lax.axis_index("occ"), lax.axis_index("vir")
    _, vcol, rank = orbitals(vir_ref)
    occ = occ_ref[...].astype(F32)
    irr_j = to_column(occ).astype(I32)
    sym_ab = pair_lanes(vcol, v * width, nvir, width)
    total = (own_ref[...] + near_ref[...] + far_ref[...]).T
    split = pieces(total, 3)
    n = total.shape[1]
    lane = iota((1, width * nvir), 1)
    rank_lanes = pick_lanes(rank, lane % nvir).astype(I32)
    row = iota((n, width * nvir), 0)
    open_ = jnp.logical_and((row // RANKS) % width == lane // nvir, row % RANKS == rank_lanes)
    for ii in range(oi):
        wide = jnp.where(jnp.logical_and(open_, row // (width * RANKS) == ii), 1.0, 0.0).astype(BF16)
        full = sum(dot(part, wide) for part in split)
        irr_i = pick_rows(occ, jnp.full((1, 1), o * oi + ii, I32)).astype(I32)
        keep = jnp.bitwise_xor(irr_j, irr_i) == sym_ab
        out_ref[ii * nocc:(ii + 1) * nocc, :] = jnp.where(keep, full, 0.0)


def spec(space):
    return pl.BlockSpec(memory_space=space)


def call(kernel, outs, ins, flops, interpret, space=pltpu.VMEM, scratch=()):
    moved = sum(x.size * 4 for x in ins) + sum(x.size * 4 for x in outs)
    return pl.pallas_call(
        kernel,
        out_shape=outs,
        in_specs=[spec(space)] * len(ins),
        out_specs=[spec(pltpu.VMEM)] * len(outs),
        scratch_shapes=scratch,
        compiler_params=pltpu.CompilerParams(vmem_limit_bytes=VMEM),
        cost_estimate=pl.CostEstimate(flops=flops, bytes_accessed=moved, transcendentals=0),
        interpret=interpret,
    )(*ins)


def pinned(x):
    return pltpu.with_memory_space_constraint(x, pltpu.HBM)


def array(*shape):
    return jax.ShapeDtypeStruct(shape, F32)


def body(nvirdev, interpret, amplitudes, integrals, occ_irrep, vir_irrep, tile_map):
    nocc, nvir = occ_irrep.shape[0], vir_irrep.shape[0]
    oi = amplitudes.shape[0] // nocc
    cdr = amplitudes.shape[1]
    width = cdr // nvir
    cm = width * RANKS
    n = nvir * RANKS
    occ = occ_irrep.reshape(1, nocc)
    vir = vir_irrep.reshape(1, nvir)

    def swap(x, k):
        return lax.ppermute(x, "vir", [(i, i ^ k) for i in range(nvirdev)])

    scratch = [
        pltpu.VMEM(amplitudes.shape, F32),
        pltpu.VMEM((1, nocc), I32),
        pltpu.VMEM((1, nvir), I32),
        pltpu.SMEM(tile_map.shape, I32),
        pltpu.VMEM((nocc, oi * cm), F32),
        pltpu.SemaphoreType.DMA((oi + 3,)),
    ]
    ins = [pinned(x) for x in (amplitudes, occ, vir, tile_map)]
    half = array(nocc // 2, oi * cm)
    own, stay, hop = call(amps_kernel, [array(nocc, oi * cm), half, half], ins, 10**9, interpret, pltpu.HBM, scratch)
    devices = nocc // oi
    hop = lax.ppermute(hop, "occ", [(i, (i + devices // 2) % devices) for i in range(devices)])
    scratch = [
        pltpu.VMEM(integrals.shape, F32),
        pltpu.VMEM((1, nvir), I32),
        pltpu.VMEM((n, integrals.shape[1]), BF16),
        pltpu.VMEM(integrals.shape, BF16),
        pltpu.VMEM(integrals.shape, BF16),
        pltpu.SemaphoreType.DMA((integrals.shape[1] // CHUNK + 1,)),
    ]
    outs = [array(n // PAIR, CLASSES * cm)] * 2
    keep, give = call(panel_kernel, outs, [pinned(integrals), pinned(vir)], 4 * 10**9, interpret, pltpu.HBM, scratch)
    stay, keep = lax.optimization_barrier((stay, keep))
    given = swap(give, 2)

    (send,) = call(functools.partial(merge_kernel, oi), [array(nocc, oi * cm)], [stay, hop], 10**6, interpret)
    halves = [list(range(devices // 2)), list(range(devices // 2, devices))]
    got = lax.all_to_all(send.reshape(devices // 2, 2 * oi, oi * cm), "occ", 0, 0, axis_index_groups=halves)
    got = got.reshape(nocc, oi * cm)


    one = array(oi * cm, nocc)
    scratch = [pltpu.VMEM((nocc, oi * cm), F32)]
    (anti,) = call(functools.partial(antisym_kernel, oi), [one], [own, got], 10**6, interpret, scratch=scratch)
    pair = [anti, swap(anti, 2), keep, given, occ]
    two = [array(2, oi * cm, nocc)] * 2
    mine, mate = call(functools.partial(ladder_kernel, oi, 1), two, pair, 10**9, interpret)
    far, farther = call(join_kernel, [one] * 2, [mine, swap(mate, 1)], 10**6, interpret)
    mine, mate = call(functools.partial(ladder_kernel, oi, 0), two, [*pair, far], 10**9, interpret)
    total, near = call(join_kernel, [one] * 2, [mine, swap(mate, 1)], 10**6, interpret)
    (far,) = call(far_kernel, [one], [far, swap(farther, 4)], 10**6, interpret)
    far, near = swap(far, 8), swap(near, 4)
    (out,) = call(
        functools.partial(spread_kernel, oi), [array(*amplitudes.shape)], [total, near, far, occ, vir], 10**9, interpret
    )
    return out


def solution(mesh, interpret=False):
    placed = (P("occ", "vir"), P("vir", None), P(), P(), P("occ", "vir"))
    return jax.shard_map(
        functools.partial(body, mesh.shape["vir"], interpret),
        mesh=mesh,
        in_specs=placed,
        out_specs=P("occ", "vir"),
        check_vma=False,
    )
```

```python
import functools

import jax
import jax.numpy as jnp
from jax import lax
from jax.experimental import pallas as pl
from jax.experimental.pallas import tpu as pltpu
from jax.sharding import PartitionSpec as P

F32, BF16, I32 = jnp.float32, jnp.bfloat16, jnp.int32
CLASSES = 8
RANKS = 8
PAIR = 2
CHUNK = 512
VMEM = 48 * 1024 * 1024


def iota(shape, dim):
    return lax.broadcasted_iota(I32, shape, dim)


def pieces(value, count):
    out = []
    for step in range(count):
        part = value.astype(BF16)
        out.append(part)
        if step + 1 < count:
            value = value - part.astype(F32)
    return out


def dot(a, b):
    return lax.dot_general(a, b, (((1,), (0,)), ((), ())), preferred_element_type=F32)


def dot_nt(a, b):
    return lax.dot_general(a, b, (((1,), (1,)), ((), ())), preferred_element_type=F32)


def to_column(row):
    n = row.shape[1]
    return jnp.sum(jnp.where(iota((n, n), 0) == iota((n, n), 1), row, 0.0), axis=1, keepdims=True)


def pick_lanes(column, index):
    shape = (column.shape[0], index.shape[1])
    return jnp.sum(jnp.where(iota(shape, 0) == index, column, 0.0), axis=0, keepdims=True)


def pick_rows(row, index):
    shape = (index.shape[0], row.shape[1])
    return jnp.sum(jnp.where(iota(shape, 1) == index, row, 0.0), axis=1, keepdims=True)


def orbitals(vir_ref):
    row = vir_ref[...].astype(F32)
    col = to_column(row)
    n = row.shape[1]
    below = jnp.logical_and(col == row, iota((n, n), 1) < iota((n, n), 0))
    rank = jnp.sum(jnp.where(below, 1.0, 0.0), axis=1, keepdims=True)
    return row, col, rank


def pair_lanes(col, first, nvir, width):
    lane = iota((1, width * nvir), 1)
    one = pick_lanes(col, first + lane // nvir).astype(I32)
    two = pick_lanes(col, lane % nvir).astype(I32)
    return jnp.bitwise_xor(one, two)


def amps_kernel(amp_hbm, occ_hbm, vir_hbm, tile_hbm, own_ref, stay_ref, hop_ref, amp_ref, occ_ref, vir_ref, tile_ref, send_ref, sems):
    nocc, nvir = occ_ref.shape[1], vir_ref.shape[1]
    width = amp_ref.shape[1] // nvir
    oi = amp_ref.shape[0] // nocc
    small = [
        pltpu.make_async_copy(a, b, sems.at[oi + k])
        for k, (a, b) in enumerate(((vir_hbm, vir_ref), (occ_hbm, occ_ref), (tile_hbm, tile_ref)))
    ]
    blocks = [
        pltpu.make_async_copy(amp_hbm.at[pl.ds(k * nocc, nocc)], amp_ref.at[pl.ds(k * nocc, nocc)], sems.at[k])
        for k in range(oi)
    ]
    for copy in small + blocks:
        copy.start()
    for copy in small:
        copy.wait()
    o, v = lax.axis_index("occ"), lax.axis_index("vir")
    _, vcol, rank = orbitals(vir_ref)
    occ = occ_ref[...].astype(F32)
    irr_j = to_column(occ).astype(I32)
    sym_cd = pair_lanes(vcol, v * width, nvir, width)
    lane = iota((1, width * nvir), 1)
    tiles = tile_ref.shape[1]
    tile = jnp.zeros_like(lane)
    for t in range(tiles):
        tile = jnp.where(lane // (width * nvir // tiles) == t, tile_ref[0, t], tile)
    sym_cd = jnp.where(tile == 1, sym_cd, -1)
    cdr, n = width * nvir, oi * width * RANKS
    rank_rows = jnp.concatenate([rank] * width, axis=0).astype(I32)
    col = iota((cdr, n), 1)
    squeeze = jnp.logical_and((col // RANKS) % width == iota((cdr, n), 0) // nvir, col % RANKS == rank_rows)
    squeeze = jnp.where(squeeze, 1.0, 0.0).astype(BF16)
    lanes = iota((nocc, n), 1) // (width * RANKS)
    own = jnp.zeros((nocc, n), F32)
    for ii in range(oi):
        irr_i = pick_rows(occ, jnp.full((1, 1), o * oi + ii, I32)).astype(I32)
        keep = jnp.bitwise_xor(irr_j, irr_i) == sym_cd
        blocks[ii].wait()
        block = jnp.where(keep, amp_ref[ii * nocc:(ii + 1) * nocc, :], 0.0)
        short = sum(dot(part, squeeze) for part in pieces(block, 3))
        own = jnp.where(lanes == ii, short, own)
    own_ref[...] = own
    devices = nocc // oi
    lanes = iota((devices, n), 1) // (width * RANKS)
    swapped = [jnp.zeros((devices, n), F32) for _ in range(oi)]
    for jj in range(oi):
        rows = own_ref[pl.ds(jj, devices, stride=oi), :]
        for ii in range(oi):
            shift = (jj - ii) % oi * (width * RANKS)
            moved = pltpu.roll(rows, shift, 1) if shift else rows
            swapped[ii] = jnp.where(lanes == jj, moved, swapped[ii])
    for ii in range(oi):
        send_ref[pl.ds(ii, devices, stride=oi), :] = swapped[ii]
    rows = nocc // 2
    high = o // (devices // 2)
    stay_ref[...] = jnp.where(high == 0, send_ref[:rows, :], send_ref[rows:, :])
    hop_ref[...] = jnp.where(high == 0, send_ref[rows:, :], send_ref[:rows, :])


def panel_kernel(int_hbm, vir_hbm, keep_ref, send_ref, int_ref, vir_ref, fold_ref, high_ref, low_ref, sems):
    nvir = vir_ref.shape[1]
    cdr = int_ref.shape[0]
    steps = int_ref.shape[1] // CHUNK
    width = cdr // nvir
    first = pltpu.make_async_copy(vir_hbm, vir_ref, sems.at[steps])
    first.start()
    copies = [
        pltpu.make_async_copy(int_hbm.at[:, pl.ds(q * CHUNK, CHUNK)], int_ref.at[:, pl.ds(q * CHUNK, CHUNK)], sems.at[q])
        for q in range(steps)
    ]
    for copy in copies:
        copy.start()
    v = lax.axis_index("vir")
    first.wait()
    vrow, vcol, rank = orbitals(vir_ref)
    row = iota((cdr, 1), 0)
    sym_rows = jnp.bitwise_xor(pick_rows(vrow, v * width + row // nvir).astype(I32), pick_rows(vrow, row % nvir).astype(I32))
    lane = iota((1, CHUNK), 1)
    b = lane % nvir
    sym_b, rank_b = pick_lanes(vcol, b).astype(I32), pick_lanes(rank, b).astype(I32)
    n = nvir * RANKS
    cm = width * RANKS
    col = iota((n, 1), 0)
    code = ((col // cm) % 4 // 2 * 4 + (col // cm) // 4 % 2 * 8 + (col // cm) % 2 + col // (n // PAIR) * 2) ^ v
    code = code * cm + col % cm
    for q in range(steps):
        a = q * (CHUNK // nvir) + lane // nvir
        sym_ab = jnp.bitwise_xor(pick_lanes(vcol, a).astype(I32), sym_b)
        sym_ab = jnp.where(a == b, -1, sym_ab)
        plus = a * RANKS + rank_b
        minus = b * RANKS + pick_lanes(rank, a).astype(I32)
        at = slice(q * CHUNK, (q + 1) * CHUNK)
        fold_ref[:, at] = jnp.where(code == plus, 1.0, jnp.where(code == minus, -1.0, 0.0)).astype(BF16)
        copies[q].wait()
        high, low = pieces(jnp.where(sym_rows == sym_ab, int_ref[:, at], 0.0), 2)
        high_ref[:, at] = high
        low_ref[:, at] = low
    total = dot_nt(fold_ref[...], high_ref[...]) + dot_nt(fold_ref[...], low_ref[...])
    k = CLASSES * cm
    new = iota((cdr, k), 1)
    rank_rows = jnp.concatenate([rank] * width, axis=0).astype(I32)
    order = jnp.logical_and(new // cm == sym_rows, (new // RANKS) % width == row // nvir)
    order = jnp.logical_and(order, new % RANKS == rank_rows)
    order = jnp.where(order, 1.0, 0.0).astype(BF16)
    placed = sum(dot(piece, order) for piece in pieces(total, 2))
    keep_ref[...] = placed[:n // PAIR, :]
    send_ref[...] = placed[n // PAIR:, :]


def merge_kernel(oi, stay_ref, hop_ref, out_ref):
    half = stay_ref.shape[0] // oi
    for k, ref in enumerate((stay_ref, hop_ref)):
        for b in range(oi):
            out_ref[pl.ds(k * oi + b, half, stride=2 * oi), :] = ref[pl.ds(b, half, stride=oi), :]


def antisym_kernel(oi, own_ref, got_ref, out_ref, diff_ref):
    rows = own_ref.shape[0] // 2
    half = rows // oi
    high = lax.axis_index("occ") // half
    for b in range(oi):
        same = got_ref[pl.ds(b, half, stride=2 * oi), :]
        other = got_ref[pl.ds(oi + b, half, stride=2 * oi), :]
        for h in range(2):
            at = pl.ds(h * rows + b, half, stride=oi)
            diff_ref[at, :] = own_ref[at, :] - jnp.where(high == h, same, other)
    out_ref[...] = diff_ref[...].T


def ladder_kernel(oi, one_ref, two_ref, keep_ref, got_ref, occ_ref, mine_ref, mate_ref):
    nocc = occ_ref.shape[1]
    o = lax.axis_index("occ")
    occ = occ_ref[...].astype(F32)
    cm = one_ref.shape[0] // oi
    stacked = []
    for ref in (keep_ref, got_ref):
        high, low = pieces(ref[...], 2)
        stacked.append((jnp.concatenate([high, low], axis=0), high))
    n = keep_ref.shape[0]
    for ii in range(oi):
        irr_i = pick_rows(occ, jnp.full((1, 1), o * oi + ii, I32)).astype(I32)
        sym = jnp.bitwise_xor(occ_ref[...], irr_i)
        total = jnp.zeros((n, nocc), F32)
        at = slice(ii * cm, (ii + 1) * cm)
        for ref, (both, high) in zip((one_ref, two_ref), stacked, strict=True):
            block = ref[at, :]
            spread = jnp.concatenate([jnp.where(sym == s, block, 0.0) for s in range(CLASSES)], axis=0)
            upper, lower = pieces(spread, 2)
            first = dot(both, upper)
            total = total + (first[:n, :] + (first[n:, :] + dot(high, lower)))
        for k in range(n // (2 * cm)):
            mine_ref[k, at, :] = total[2 * k * cm:(2 * k + 1) * cm, :]
            mate_ref[k, at, :] = total[(2 * k + 1) * cm:(2 * k + 2) * cm, :]


def join_kernel(mine_ref, mate_ref, *outs):
    for k, out in enumerate(outs):
        out[...] = mine_ref[k] + mate_ref[k]


def far_kernel(far_ref, got_ref, out_ref):
    out_ref[...] = far_ref[...] + got_ref[...]


def near_kernel(near_ref, after_ref, out_ref):
    del after_ref
    out_ref[...] = near_ref[...]


def spread_kernel(oi, own_ref, near_ref, far_ref, occ_ref, vir_ref, out_ref):
    nocc, nvir = occ_ref.shape[1], vir_ref.shape[1]
    width = out_ref.shape[1] // nvir
    o, v = lax.axis_index("occ"), lax.axis_index("vir")
    _, vcol, rank = orbitals(vir_ref)
    occ = occ_ref[...].astype(F32)
    irr_j = to_column(occ).astype(I32)
    sym_ab = pair_lanes(vcol, v * width, nvir, width)
    total = (own_ref[...] + near_ref[...] + far_ref[...]).T
    split = pieces(total, 3)
    n = total.shape[1]
    lane = iota((1, width * nvir), 1)
    rank_lanes = pick_lanes(rank, lane % nvir).astype(I32)
    row = iota((n, width * nvir), 0)
    open_ = jnp.logical_and((row // RANKS) % width == lane // nvir, row % RANKS == rank_lanes)
    for ii in range(oi):
        wide = jnp.where(jnp.logical_and(open_, row // (width * RANKS) == ii), 1.0, 0.0).astype(BF16)
        full = sum(dot(part, wide) for part in split)
        irr_i = pick_rows(occ, jnp.full((1, 1), o * oi + ii, I32)).astype(I32)
        keep = jnp.bitwise_xor(irr_j, irr_i) == sym_ab
        out_ref[ii * nocc:(ii + 1) * nocc, :] = jnp.where(keep, full, 0.0)


def spec(space):
    return pl.BlockSpec(memory_space=space)


def call(kernel, outs, ins, flops, interpret, space=pltpu.VMEM, scratch=()):
    moved = sum(x.size * 4 for x in ins) + sum(x.size * 4 for x in outs)
    return pl.pallas_call(
        kernel,
        out_shape=outs,
        in_specs=[spec(space)] * len(ins),
        out_specs=[spec(pltpu.VMEM)] * len(outs),
        scratch_shapes=scratch,
        compiler_params=pltpu.CompilerParams(vmem_limit_bytes=VMEM),
        cost_estimate=pl.CostEstimate(flops=flops, bytes_accessed=moved, transcendentals=0),
        interpret=interpret,
    )(*ins)


def pinned(x):
    return pltpu.with_memory_space_constraint(x, pltpu.HBM)


def array(*shape):
    return jax.ShapeDtypeStruct(shape, F32)


def body(nvirdev, interpret, amplitudes, integrals, occ_irrep, vir_irrep, tile_map):
    nocc, nvir = occ_irrep.shape[0], vir_irrep.shape[0]
    oi = amplitudes.shape[0] // nocc
    cdr = amplitudes.shape[1]
    width = cdr // nvir
    cm = width * RANKS
    n = nvir * RANKS
    occ = occ_irrep.reshape(1, nocc)
    vir = vir_irrep.reshape(1, nvir)

    def swap(x, k):
        return lax.ppermute(x, "vir", [(i, i ^ k) for i in range(nvirdev)])

    scratch = [
        pltpu.VMEM(amplitudes.shape, F32),
        pltpu.VMEM((1, nocc), I32),
        pltpu.VMEM((1, nvir), I32),
        pltpu.SMEM(tile_map.shape, I32),
        pltpu.VMEM((nocc, oi * cm), F32),
        pltpu.SemaphoreType.DMA((oi + 3,)),
    ]
    ins = [pinned(x) for x in (amplitudes, occ, vir, tile_map)]
    half = array(nocc // 2, oi * cm)
    own, stay, hop = call(amps_kernel, [array(nocc, oi * cm), half, half], ins, 10**9, interpret, pltpu.HBM, scratch)
    devices = nocc // oi
    hop = lax.ppermute(hop, "occ", [(i, (i + devices // 2) % devices) for i in range(devices)])
    scratch = [
        pltpu.VMEM(integrals.shape, F32),
        pltpu.VMEM((1, nvir), I32),
        pltpu.VMEM((n, integrals.shape[1]), BF16),
        pltpu.VMEM(integrals.shape, BF16),
        pltpu.VMEM(integrals.shape, BF16),
        pltpu.SemaphoreType.DMA((integrals.shape[1] // CHUNK + 1,)),
    ]
    outs = [array(n // PAIR, CLASSES * cm)] * 2
    keep, give = call(panel_kernel, outs, [pinned(integrals), pinned(vir)], 4 * 10**9, interpret, pltpu.HBM, scratch)
    stay, keep = lax.optimization_barrier((stay, keep))
    given = swap(give, 2)

    (send,) = call(functools.partial(merge_kernel, oi), [array(nocc, oi * cm)], [stay, hop], 10**6, interpret)
    halves = [list(range(devices // 2)), list(range(devices // 2, devices))]
    got = lax.all_to_all(send.reshape(devices // 2, 2 * oi, oi * cm), "occ", 0, 0, axis_index_groups=halves)
    got = got.reshape(nocc, oi * cm)


    one = array(oi * cm, nocc)
    scratch = [pltpu.VMEM((nocc, oi * cm), F32)]
    (anti,) = call(functools.partial(antisym_kernel, oi), [one], [own, got], 10**6, interpret, scratch=scratch)
    far = nvirdev // 4
    mine, mate = call(
        functools.partial(ladder_kernel, oi),
        [array(far, oi * cm, nocc)] * 2,
        [anti, swap(anti, 2), keep, given, occ],
        2 * 10**9,
        interpret,
    )
    sums = call(join_kernel, [one] * far, [mine, swap(mate, 1)], 10**6, interpret)
    (far,) = call(far_kernel, [one], [sums[2], swap(sums[3], 4)], 10**6, interpret)
    (near,) = call(near_kernel, [one], [sums[1], far], 10**10, interpret)
    far, near = swap(far, 8), swap(near, 4)
    (out,) = call(
        functools.partial(spread_kernel, oi), [array(*amplitudes.shape)], [sums[0], near, far, occ, vir], 10**9, interpret
    )
    return out


def solution(mesh, interpret=False):
    placed = (P("occ", "vir"), P("vir", None), P(), P(), P("occ", "vir"))
    return jax.shard_map(
        functools.partial(body, mesh.shape["vir"], interpret),
        mesh=mesh,
        in_specs=placed,
        out_specs=P("occ", "vir"),
        check_vma=False,
    )
```
